256 devices in a mesh: lat: 16 (over y, x_hi, core), lon: 16 (over x_lo, z).
Axes of the slice: x: 4 (x_hi: 2, x_lo: 2; x = x_hi * 2 + x_lo), y: 4, z: 8, core: 2. Of those that a mesh axis runs over, the one named last changes fastest.
Arguments:
- features: bfloat16 [384, 720, 256], P('lat', 'lon'), may hold values from -6 to 6
- obs_mask: int32 [384, 720, 8], P('lat', 'lon'), may hold values 0 or 1
- filter_taps: bfloat16 [384, 4, 3, 17], replicated, may hold values from 0.049804688 to 1
- band_width: int32 [384], replicated, may hold values from 1 to 8, as said below
- mixing: bfloat16 [8, 4, 32, 32], replicated, may hold values from -0.5 to 0.5
- cotangent: bfloat16 [384, 720, 256], P('lat', 'lon'), may hold values from -6 to 6
Outputs:
- infilled: bfloat16 [384, 720, 256], P('lat', 'lon')
- input_grad: bfloat16 [384, 720, 256], P('lat', 'lon')
- weight_grad: float32 [8, 4, 32, 32], replicated
The draws below stay inside these ranges and needn't reach their ends.
Inputs may be any that keep to these rules, and one draw needn't show every extreme that they name: band_width is 8 at the first and last cycle and 1 at cycle 384 // 2.
All inputs are finite; a program needn't handle non-finite values. No bound on the sum of `obs_mask` on one device may be relied on, other than what follows from the above.
Results may differ from the reference program's by a relative error of at most 0.005.
Values may be sent and summed in bfloat16 or wider, within the bound.
A program may use at most 128 MiB of HBM per device.

```python
import math
import jax
import jax.numpy as jnp
from jax import lax

C = 256
G = 8
B = 4
H = 8
LAT_DEV = 24
CG = 32
NLAT = 384
NLON = 720
N_LAT = 16


def draw_band_width(key, part):
    cycle_index = jnp.arange(NLAT, dtype=jnp.int32)
    distance = jnp.abs(2 * cycle_index - (NLAT - 1))
    baseline = 1 + (H - 1) * distance // max(NLAT - 1, 1)
    jitter = jax.random.randint(key, (NLAT,), -1, 2)
    widths = jnp.clip(baseline + jitter, 1, H)
    widths = widths.at[0].set(H).at[NLAT - 1].set(H).at[NLAT // 2].set(1)
    return widths.astype(jnp.int32)


def place_ends(entries, key, least, high):
    longest = entries.shape.index(max(entries.shape))
    spots = []
    for shift in (0, 1):
        where = [jax.random.randint(jax.random.fold_in(key, axis), (), 0, length) for axis, length in enumerate(entries.shape)]
        where[longest] = (where[longest] + shift) % entries.shape[longest]
        spots.append(tuple(where))
    return entries.at[spots[0]].set(least).at[spots[1]].set(high)


def shard_levels(stream_key, extent, cuts, low, high):
    gain, own = 1.0, jax.random.fold_in(stream_key, 6)
    for position, blocks in cuts:
        heights = jnp.exp(jax.random.uniform(jax.random.fold_in(own, position), (blocks,), jnp.float32, low / len(cuts), high / len(cuts)))
        gain = gain * jnp.repeat(heights, extent[position] // blocks).reshape([-1 if axis == position else 1 for axis in range(len(extent))])
    return gain


def bell_draw(key, dims, width, limit, cuts=(), kind=jnp.bfloat16):
    factor_of = shard_levels(key, dims, cuts, -0.22, 0.18) if cuts else 1.0
    drawn = jax.random.normal(key, dims, jnp.float32) * width * factor_of
    return jnp.minimum(jnp.maximum(drawn, -limit), limit).astype(kind)


def setup_inputs(seed: int = 0) -> dict:
    key_of = jax.random.split(jax.random.key(seed), 7)
    return {
        "features": bell_draw(key_of[0], (NLAT, NLON, C), 1.0, 6.0, ((0, 16), (1, 16))),
        "obs_mask": place_ends((jax.random.randint(key_of[1], (NLAT, NLON, G), 0, 2) < 1).astype(jnp.int32), jax.random.fold_in(key_of[1], 1), 0, 1),
        "filter_taps": jnp.clip(jnp.exp(jax.random.uniform(key_of[2], (NLAT, B, 3, 2 * H + 1), jnp.float32, math.log(0.049804688), math.log(1.0))), 0.049804688, 1.0).astype(jnp.bfloat16),
        "band_width": draw_band_width(jax.random.fold_in(key_of[6], 71), 0),
        "mixing": bell_draw(key_of[4], (G, B, CG, CG), (B * CG) ** -0.5, 0.5),
        "cotangent": bell_draw(key_of[5], (NLAT, NLON, C), 1.0, 6.0, ((0, 16), (1, 16))),
    }


def wrap_pad(values):
    widened = jnp.concatenate([values[:, NLON - H:], values, values[:, :H]], axis=1)
    return jnp.pad(widened, ((1, 1), (0, 0), (0, 0)))

def reference(features, obs_mask, filter_taps, band_width, mixing, cotangent):
    mask_float = obs_mask.astype(jnp.float32)
    masked = (features.astype(jnp.float32).reshape(NLAT, NLON, G, CG) * mask_float[..., None]).reshape(NLAT, NLON, C)
    offsets = jnp.arange(2 * H + 1) - H
    allowed = (jnp.abs(offsets)[None, :] <= band_width[:, None]).astype(jnp.float32)
    taps = filter_taps.astype(jnp.float32) * allowed[:, None, None, :]
    taps_pad = jnp.pad(taps, ((1, 1), (0, 0), (0, 0), (0, 0)))
    upstream = cotangent.astype(jnp.float32).reshape(NLAT, NLON, G, CG)
    masked_pad = wrap_pad(masked)
    mask_pad = wrap_pad(mask_float)
    starts = jnp.arange(N_LAT, dtype=jnp.int32) * LAT_DEV
    output_sum = jnp.zeros((NLAT, NLON, G, CG), jnp.float32)
    adjoint_sum = jnp.zeros((NLAT, NLON, C), jnp.float32)
    grad_list = []
    for basis in range(B):
        basis_mix = mixing[:, basis].astype(jnp.float32)
        basis_taps = taps[:, basis]
        padded_taps = taps_pad[:, basis]

        def forward_block(start):
            rows_in = lax.dynamic_slice_in_dim(masked_pad, start, LAT_DEV + 2, 0)
            rows_mask = lax.dynamic_slice_in_dim(mask_pad, start, LAT_DEV + 2, 0)
            block_taps = lax.dynamic_slice_in_dim(basis_taps, start, LAT_DEV, 0)
            up_rows = lax.dynamic_slice_in_dim(upstream, start, LAT_DEV, 0)
            numerator = jnp.zeros((LAT_DEV, NLON, C), jnp.float32)
            denominator = jnp.zeros((LAT_DEV, NLON, G), jnp.float32)
            for lat_step in range(3):
                for lon_step in range(2 * H + 1):
                    weight_col = block_taps[:, lat_step, lon_step][:, None, None]
                    numerator = numerator + weight_col * rows_in[lat_step:lat_step + LAT_DEV, lon_step:lon_step + NLON]
                    denominator = denominator + weight_col * rows_mask[lat_step:lat_step + LAT_DEV, lon_step:lon_step + NLON]
            safe_denom = jnp.maximum(denominator, 1.0)
            scaled = (numerator.reshape(LAT_DEV, NLON, G, CG) / safe_denom[..., None]).astype(jnp.bfloat16)
            scaled = lax.optimization_barrier(scaled).astype(jnp.float32)
            block_out = jnp.einsum('ijgc,gco->ijgo', scaled, basis_mix)
            block_grad = jnp.einsum('ijgc,ijgo->gco', scaled, up_rows)
            back_prop = jnp.einsum('ijgo,gco->ijgc', up_rows, basis_mix)
            pulled = (back_prop / safe_denom[..., None]).astype(jnp.bfloat16)
            pulled = lax.optimization_barrier(pulled).astype(jnp.float32).reshape(LAT_DEV, NLON, C)
            return (block_out, block_grad, pulled)
        block_outs, block_grads, pulled_all = lax.map(forward_block, starts)
        output_sum = output_sum + block_outs.reshape(NLAT, NLON, G, CG)
        grad_list.append(lax.optimization_barrier(jnp.sum(block_grads, axis=0)))
        pulled_pad = wrap_pad(pulled_all.reshape(NLAT, NLON, C))

        def adjoint_block(start):
            rows_grad = lax.dynamic_slice_in_dim(pulled_pad, start, LAT_DEV + 2, 0)
            rows_taps = lax.dynamic_slice_in_dim(padded_taps, start, LAT_DEV + 2, 0)
            total = jnp.zeros((LAT_DEV, NLON, C), jnp.float32)
            for lat_step in range(3):
                first = 2 - lat_step
                for lon_step in range(2 * H + 1):
                    column = 2 * H - lon_step
                    weight_col = rows_taps[first:first + LAT_DEV, lat_step, lon_step][:, None, None]
                    total = total + weight_col * rows_grad[first:first + LAT_DEV, column:column + NLON]
            return total
        adjoint_sum = adjoint_sum + lax.map(adjoint_block, starts).reshape(NLAT, NLON, C)
    infilled = output_sum.reshape(NLAT, NLON, C).astype(jnp.bfloat16)
    weight_grad = jnp.stack(grad_list, axis=1) / jnp.sqrt(jnp.float32(NLAT * NLON))
    input_grad = (adjoint_sum.reshape(NLAT, NLON, G, CG) * mask_float[..., None]).reshape(NLAT, NLON, C).astype(jnp.bfloat16)
    return (infilled, input_grad, weight_grad)
```

```python
import functools
import math

import jax
import jax.numpy as jnp
from jax import lax
from jax.experimental import pallas as pl
from jax.experimental.pallas import tpu as pltpu
from jax.sharding import PartitionSpec as P

MESH = pl.DeviceIdType.MESH
F32 = jnp.float32
BF16 = jnp.bfloat16
ROWS = 24
COLS = 45
PADC = 48
SLOT = 64
CHAN = 256
GROUPS = 8
WIDTH = 32
BASES = 4
REACH = 8
TAPS = 2 * REACH + 1
PAIRS = ROWS // 2
BAND = 2 * BASES * PADC


def iota(shape, dim):
    return lax.broadcasted_iota(jnp.int32, shape, dim)


def one_hot(test):
    return jnp.where(test, 1.0, 0.0).astype(BF16)


def dot(a, b):
    return jnp.dot(a, b, preferred_element_type=F32)


def pad_rows(x):
    return jnp.concatenate([x, jnp.zeros((PADC - COLS, x.shape[1]), F32)], axis=0)


def kernel(
    n_lat, n_lon,
    feat, mask, base, mix, cot,
    infilled, input_grad, weight_grad,
    field, seen, cots, cots_t, mixer, band, band_t, scaled, pulled, back, total,
    send_first, send_last, from_right, from_left, corners,
    share, got_lon, got_lat, final,
    part_right, part_left, part_top, part_bottom, part_corner,
    halo_send, halo_recv, part_send, part_recv, sum_send, sum_recv,
):
    la, lo = lax.axis_index("lat"), lax.axis_index("lon")
    up, down = lax.rem(la + n_lat - 1, n_lat), lax.rem(la + 1, n_lat)
    left, right = lax.rem(lo + n_lon - 1, n_lon), lax.rem(lo + 1, n_lon)

    barrier = pltpu.get_barrier_semaphore()

    def greet(dev_lat, dev_lon):
        pl.semaphore_signal(
            barrier, inc=1, device_id=(dev_lat, dev_lon), device_id_type=MESH
        )

    @pl.loop(1, n_lon)
    def _(d):
        greet(la, lax.rem(lo + d, n_lon))

    @pl.loop(1, n_lat)
    def _(d):
        greet(lax.rem(la + d, n_lat), lo)

    for dev_lat in (up, down):
        for dev_lon in (left, right):
            greet(dev_lat, dev_lon)

    expand = one_hot(iota((GROUPS, CHAN), 1) // WIDTH == iota((GROUPS, CHAN), 0))
    squeeze = one_hot(iota((CHAN, 128), 0) == WIDTH * iota((CHAN, 128), 1))
    expand_wide = one_hot(iota((128, CHAN), 1) // WIDTH == iota((128, CHAN), 0))

    @pl.loop(0, PAIRS)
    def _(t):
        firsts, lasts, first_seen, last_seen = [], [], [], []
        for k in range(2):
            i = 2 * t + k
            spread = dot(mask[i].astype(F32).astype(BF16), expand)
            masked = pad_rows(feat[i].astype(F32) * spread)
            spread = pad_rows(spread)
            field[i + 1, 0:PADC] = masked.astype(BF16)
            seen[i + 1, 0:PADC] = spread.astype(BF16)
            firsts.append(masked[0:8])
            first_seen.append(spread[0:8])
            lasts.append(pltpu.roll(masked[32:48], 11, 0)[0:8])
            last_seen.append(pltpu.roll(spread[32:48], 11, 0)[0:8])
        for ref, values, flags in (
            (send_first, firsts, first_seen), (send_last, lasts, last_seen)
        ):
            ref[t, :, 0:CHAN] = jnp.concatenate(values, axis=0).astype(BF16)
            marks = dot(jnp.concatenate(flags, axis=0).astype(BF16), squeeze)
            ref[t, :, CHAN:] = marks.astype(BF16)

    pl.semaphore_wait(barrier, n_lon - 1 + n_lat - 1 + 4)

    def remote(src, dst, send, recv, dev_lat, dev_lon):
        return pltpu.make_async_remote_copy(
            src_ref=src, dst_ref=dst, send_sem=send, recv_sem=recv,
            device_id=(dev_lat, dev_lon), device_id_type=MESH,
        )

    halo_plan = (
        (send_first, from_right, la, left),
        (send_last, from_left, la, right),
        (field.at[1, pl.ds(0, PADC)], field.at[ROWS + 1, pl.ds(0, PADC)], up, lo),
        (seen.at[1, pl.ds(0, PADC)], seen.at[ROWS + 1, pl.ds(0, PADC)], up, lo),
        (field.at[ROWS, pl.ds(0, PADC)], field.at[0, pl.ds(0, PADC)], down, lo),
        (seen.at[ROWS, pl.ds(0, PADC)], seen.at[0, pl.ds(0, PADC)], down, lo),
        (send_first.at[0], corners.at[0], up, left),
        (send_last.at[0], corners.at[1], up, right),
        (send_first.at[PAIRS - 1], corners.at[2], down, left),
        (send_last.at[PAIRS - 1], corners.at[3], down, right),
    )
    halos = [
        remote(src, dst, halo_send.at[n], halo_recv.at[n], dev_lat, dev_lon)
        for n, (src, dst, dev_lat, dev_lon) in enumerate(halo_plan)
    ]
    for copy in halos:
        copy.start()

    lane = iota((PADC, 128), 1) % SLOT

    @pl.loop(0, PAIRS)
    def _(t):
        for k in range(2):
            taps = base[2 * t + k]
            for b in range(BASES):
                for v in range(2):
                    line = taps[b : b + 1, v * 128 : v * 128 + 128]
                    row = jnp.broadcast_to(line, (PADC, 128))
                    late = pltpu.roll(jnp.broadcast_to(line, (8, 128)), 3, 1)
                    late = jnp.concatenate([late, late], axis=0)
                    own = pltpu.roll(row, 120, 1, stride=1, stride_axis=0)
                    high = pltpu.roll(late, 24, 1, stride=1, stride_axis=0)
                    low = pltpu.roll(row[0:8], 56, 1, stride=1, stride_axis=0)
                    piece = jnp.concatenate(
                        [
                            jnp.where(
                                lane[0:8] < COLS, own[0:8], jnp.where(lane[0:8] < 56, 0.0, low)
                            ),
                            own[8:32],
                            jnp.where(
                                lane[0:16] < COLS,
                                own[32:48],
                                jnp.where(
                                    (lane[0:16] >= PADC) & (lane[0:16] < 56), high, 0.0
                                ),
                            ),
                        ],
                        axis=0,
                    )
                    start = (k * BASES + b) * PADC
                    band[t, start : start + PADC, v * 128 : v * 128 + 128] = piece.astype(BF16)
        band_t[t] = band[t].T

    repeat = one_hot(iota((WIDTH, CHAN), 1) % WIDTH == iota((WIDTH, CHAN), 0))
    block = iota((CHAN, CHAN), 0) // WIDTH == iota((CHAN, CHAN), 1) // WIDTH
    for b in range(BASES):
        tall = mix[:, b].reshape(CHAN, WIDTH)
        mixer[b] = jnp.where(block, dot(tall, repeat), 0.0).astype(BF16)

    @pl.loop(0, ROWS)
    def _(i):
        start = pl.multiple_of(i * PADC, PADC)
        cots[pl.ds(start, PADC)] = pad_rows(cot[i].astype(F32)).astype(BF16)

    for n in range(ROWS * PADC // 128):
        cots_t[:, n * 128 : n * 128 + 128] = cots[n * 128 : n * 128 + 128].T

    @pl.loop(0, PAIRS // 4)
    def _(n):
        start = pl.multiple_of(n * 8 * PADC, 8 * PADC)
        rows = cots[pl.ds(start, 8 * PADC)]
        for b in range(BASES):
            result = lax.dot_general(
                rows, mixer[b], (((1,), (1,)), ((), ())), preferred_element_type=F32
            )
            for i in range(8):
                first = ((i % 2) * BASES + b) * PADC
                back[4 * n + i // 2, first : first + PADC] = result[i * PADC : i * PADC + PADC]

    for copy in halos:
        copy.wait_recv()

    def place(ref, i, high, low):
        ref[i, PADC:SLOT] = jnp.concatenate([high, low], axis=0).astype(BF16)

    def opened(strip):
        return strip[:, 0:CHAN].astype(F32), dot(strip[:, CHAN:], expand_wide)

    @pl.loop(0, PAIRS)
    def _(t):
        high, low = opened(from_right[t]), opened(from_left[t])
        for ref, h, l in zip((field, seen), high, low):
            place(ref, 2 * t + 1, h[0:8], l[0:8])
            place(ref, 2 * t + 2, h[8:16], l[8:16])

    for i, h_slot, l_slot, rows in ((ROWS + 1, 0, 1, slice(0, 8)), (0, 2, 3, slice(8, 16))):
        for ref, h, l in zip((field, seen), opened(corners[h_slot]), opened(corners[l_slot])):
            place(ref, i, h[rows], l[rows])

    @pl.loop(0, PAIRS)
    def _(t):
        weights = band[t]
        numerator = dot(weights, field[pl.ds(2 * t, 4)].reshape(4 * SLOT, CHAN))
        denominator = dot(weights, seen[pl.ds(2 * t, 4)].reshape(4 * SLOT, CHAN))
        inverse = 1.0 / jnp.maximum(denominator, 1.0)
        normal = (numerator * inverse).astype(BF16)
        for k in range(2):
            start = pl.multiple_of((2 * t + k) * PADC, PADC)
            for b in range(BASES):
                first = (k * BASES + b) * PADC
                scaled[b, pl.ds(start, PADC)] = normal[first : first + PADC]
        pulled[t] = (back[t] * inverse).astype(BF16)

    for b in range(BASES):
        grad = jnp.where(block, dot(cots_t[...], scaled[b]), 0.0)
        share[b * WIDTH : b * WIDTH + WIDTH] = jnp.sum(grad.reshape(GROUPS, WIDTH, CHAN), axis=0)

    def lon_share(d):
        to = lax.rem(lo + d, n_lon)
        rows = pl.ds(pl.multiple_of(to * 8, 8), 8)
        return remote(
            share.at[rows], got_lon.at[d], sum_send.at[0, d], sum_recv.at[0, d], la, to
        )

    def lat_share(d):
        to = lax.rem(la + d, n_lat)
        return remote(
            got_lat.at[la], got_lat.at[la], sum_send.at[1, d], sum_recv.at[1, d], to, lo
        )

    def spread_share(d):
        to = lax.rem(lo + d, n_lon)
        return remote(
            final.at[lo], final.at[lo], sum_send.at[2, d], sum_recv.at[2, d], la, to
        )

    def start_all(make, count):
        @pl.loop(1, count)
        def _(d):
            make(d).start()

    def finish_all(make, count):
        @pl.loop(1, count)
        def _(d):
            make(d).wait_recv()

        @pl.loop(1, count)
        def _(d):
            make(d).wait_send()

    start_all(lon_share, n_lon)

    @pl.loop(0, PAIRS // 4)
    def _(n):
        start = pl.multiple_of(n * 8 * PADC, 8 * PADC)
        result = dot(scaled[0, pl.ds(start, 8 * PADC)], mixer[0])
        for b in range(1, BASES):
            result += dot(scaled[b, pl.ds(start, 8 * PADC)], mixer[b])
        for i in range(8):
            infilled[8 * n + i] = result[i * PADC : i * PADC + COLS].astype(BF16)

    finish_all(lon_share, n_lon)
    got_lon[0] = share[pl.ds(pl.multiple_of(lo * 8, 8), 8)]
    got_lat[la] = jnp.sum(got_lon[...], axis=0)
    start_all(lat_share, n_lat)

    total[0:2] = jnp.zeros((2, SLOT, CHAN), F32)

    @pl.loop(0, PAIRS)
    def _(t):
        result = dot(band_t[t], pulled[t]).reshape(4, SLOT, CHAN)
        total[pl.ds(2 * t, 2)] += result[0:2]
        total[pl.ds(2 * t + 2, 2)] = result[2:4]

    inner = pl.ds(1, ROWS)
    high, low, own = pl.ds(PADC, 8), pl.ds(56, 8), pl.ds(0, PADC)
    part_plan = (
        (total.at[inner, low], part_right, la, left),
        (total.at[inner, high], part_left, la, right),
        (total.at[0, own], part_bottom, up, lo),
        (total.at[ROWS + 1, own], part_top, down, lo),
        (total.at[0, low], part_corner.at[0], up, left),
        (total.at[0, high], part_corner.at[1], up, right),
        (total.at[ROWS + 1, low], part_corner.at[2], down, left),
        (total.at[ROWS + 1, high], part_corner.at[3], down, right),
    )
    parts = [
        remote(src, dst, part_send.at[n], part_recv.at[n], dev_lat, dev_lon)
        for n, (src, dst, dev_lat, dev_lon) in enumerate(part_plan)
    ]
    for copy in parts:
        copy.start()

    finish_all(lat_share, n_lat)
    final[lo] = jnp.sum(got_lat[...], axis=0) * (
        1.0 / math.sqrt(ROWS * n_lat * COLS * n_lon)
    )
    start_all(spread_share, n_lon)

    for copy in parts:
        copy.wait_recv()
    for copy in parts:
        copy.wait_send()

    part_left[0] += part_corner[3]
    part_right[0] += part_corner[2]
    part_left[ROWS - 1] += part_corner[1]
    part_right[ROWS - 1] += part_corner[0]
    total[1, 0:PADC] += part_top[...]
    total[ROWS, 0:PADC] += part_bottom[...]

    @pl.loop(0, ROWS)
    def _(i):
        tail = pltpu.roll(
            jnp.concatenate([part_right[i], jnp.zeros((8, CHAN), F32)], axis=0), 5, 0
        )
        extra = jnp.concatenate([part_left[i], jnp.zeros((24, CHAN), F32), tail], axis=0)
        result = (total[i + 1, 0:PADC] + extra) * seen[i + 1, 0:PADC].astype(F32)
        input_grad[i] = result[0:COLS].astype(BF16)

    for copy in halos:
        copy.wait_send()
    finish_all(spread_share, n_lon)
    for b in range(BASES):
        grad = final[4 * b : 4 * b + 4].reshape(WIDTH, CHAN)
        weight_grad[:, b] = grad.T.reshape(GROUPS, WIDTH, WIDTH)


def local(features, obs_mask, filter_taps, band_width, mixing, cotangent):
    n_lat, n_lon = lax.axis_size("lat"), lax.axis_size("lon")
    first = lax.axis_index("lat") * ROWS
    taps = lax.dynamic_slice_in_dim(filter_taps, first, ROWS, 0).astype(F32)
    width = lax.dynamic_slice_in_dim(band_width, first, ROWS, 0)
    inside = jnp.abs(jnp.arange(TAPS) - REACH)[None, :] <= width[:, None]
    cycle = first + jnp.arange(ROWS)[:, None] + jnp.arange(3)[None, :] - 1
    on_sphere = (cycle >= 0) & (cycle < n_lat * ROWS)
    keep = inside[:, None, None, :] & on_sphere[:, None, :, None]
    taps = jnp.where(keep, taps, 0.0)
    taps = jnp.pad(taps, ((0, 0), (0, 0), (0, 0), (0, SLOT - TAPS)))
    taps = taps.reshape(PAIRS, 2, BASES, 3 * SLOT)
    base = jnp.stack(
        [
            jnp.pad(taps[:, 0], ((0, 0), (0, 0), (0, SLOT))),
            jnp.pad(taps[:, 1], ((0, 0), (0, 0), (SLOT, 0))),
        ],
        axis=1,
    ).reshape(ROWS, BASES, 4 * SLOT)

    vmem = pl.BlockSpec(memory_space=pltpu.VMEM)
    return pl.pallas_call(
        functools.partial(kernel, n_lat, n_lon),
        out_shape=(
            jax.ShapeDtypeStruct((ROWS, COLS, CHAN), BF16),
            jax.ShapeDtypeStruct((ROWS, COLS, CHAN), BF16),
            jax.ShapeDtypeStruct((GROUPS, BASES, WIDTH, WIDTH), F32),
        ),
        in_specs=[vmem] * 5,
        out_specs=(vmem,) * 3,
        scratch_shapes=[
            pltpu.VMEM((ROWS + 2, SLOT, CHAN), BF16),
            pltpu.VMEM((ROWS + 2, SLOT, CHAN), BF16),
            pltpu.VMEM((ROWS * PADC, CHAN), BF16),
            pltpu.VMEM((CHAN, ROWS * PADC), BF16),
            pltpu.VMEM((BASES, CHAN, CHAN), BF16),
            pltpu.VMEM((PAIRS, BAND, 4 * SLOT), BF16),
            pltpu.VMEM((PAIRS, 4 * SLOT, BAND), BF16),
            pltpu.VMEM((BASES, ROWS * PADC, CHAN), BF16),
            pltpu.VMEM((PAIRS, BAND, CHAN), BF16),
            pltpu.VMEM((PAIRS, BAND, CHAN), F32),
            pltpu.VMEM((ROWS + 2, SLOT, CHAN), F32),
            pltpu.VMEM((PAIRS, 16, CHAN + 128), BF16),
            pltpu.VMEM((PAIRS, 16, CHAN + 128), BF16),
            pltpu.VMEM((PAIRS, 16, CHAN + 128), BF16),
            pltpu.VMEM((PAIRS, 16, CHAN + 128), BF16),
            pltpu.VMEM((4, 16, CHAN + 128), BF16),
            pltpu.VMEM((BASES * WIDTH, CHAN), F32),
            pltpu.VMEM((16, 8, CHAN), F32),
            pltpu.VMEM((16, 8, CHAN), F32),
            pltpu.VMEM((16, 8, CHAN), F32),
            pltpu.VMEM((ROWS, 8, CHAN), F32),
            pltpu.VMEM((ROWS, 8, CHAN), F32),
            pltpu.VMEM((PADC, CHAN), F32),
            pltpu.VMEM((PADC, CHAN), F32),
            pltpu.VMEM((4, 8, CHAN), F32),
            pltpu.SemaphoreType.DMA((10,)),
            pltpu.SemaphoreType.DMA((10,)),
            pltpu.SemaphoreType.DMA((8,)),
            pltpu.SemaphoreType.DMA((8,)),
            pltpu.SemaphoreType.DMA((3, 16)),
            pltpu.SemaphoreType.DMA((3, 16)),
        ],
        compiler_params=pltpu.CompilerParams(
            collective_id=0, has_side_effects=True, vmem_limit_bytes=50 * 1024 * 1024
        ),
    )(features, obs_mask, base, mixing, cotangent)


def solution(mesh):
    placed = (P("lat", "lon", None), P("lat", "lon", None), P(), P(), P(), P("lat", "lon", None))
    return jax.shard_map(
        local,
        mesh=mesh,
        in_specs=placed,
        out_specs=(P("lat", "lon", None), P("lat", "lon", None), P()),
        check_vma=False,
    )
```

```python
import functools
import math

import jax
import jax.numpy as jnp
from jax import lax
from jax.experimental import pallas as pl
from jax.experimental.pallas import tpu as pltpu
from jax.sharding import PartitionSpec as P

MESH = pl.DeviceIdType.MESH
F32 = jnp.float32
BF16 = jnp.bfloat16
ROWS = 24
COLS = 45
PADC = 48
SLOT = 64
CHAN = 256
GROUPS = 8
WIDTH = 32
BASES = 4
REACH = 8
TAPS = 2 * REACH + 1
PAIRS = ROWS // 2
BAND = 2 * BASES * PADC


def far_first(sizes):
    steps = [(a, b) for a in range(sizes[0]) for b in range(sizes[1])]
    hops = lambda s: sum(min(k, n - k) for k, n in zip(s, sizes))
    return sorted(steps, key=lambda s: (-hops(s), s))[:-1]


PLANE = far_first((4, 4))
LINE = far_first((2, 8))


def iota(shape, dim):
    return lax.broadcasted_iota(jnp.int32, shape, dim)


def one_hot(test):
    return jnp.where(test, 1.0, 0.0).astype(BF16)


def dot(a, b):
    return jnp.dot(a, b, preferred_element_type=F32)


def pad_rows(x):
    return jnp.concatenate([x, jnp.zeros((PADC - COLS, x.shape[1]), F32)], axis=0)


def kernel(
    n_lat, n_lon,
    feat, mask, taps, width, mix, cot,
    infilled, input_grad, weight_sum,
    feat_own, mask_own, taps_own, mix_own, cot_own,
    wide_feat, wide_cot, tap_rows, base,
    field, seen, cots, cots_t, mixer, band, scaled, pulled, inverse, total,
    from_right, from_left, marks, marks_right, marks_left, marks_corner, mark_top, mark_bottom,
    corners, share, got_plane, got_line, final,
    part_right, part_left, part_top, part_bottom, part_corner,
    load_sem, store_sem, halo_send, halo_recv, part_send, part_recv, sum_send, sum_recv,
):
    la, lo = lax.axis_index("lat"), lax.axis_index("lon")
    up, down = lax.rem(la + n_lat - 1, n_lat), lax.rem(la + 1, n_lat)
    left, right = lax.rem(lo + n_lon - 1, n_lon), lax.rem(lo + 1, n_lon)

    loads = [
        pltpu.make_async_copy(src, dst, load_sem.at[n])
        for n, (src, dst) in enumerate(
            (
                (mask, mask_own), (feat, feat_own), (taps, taps_own),
                (cot, cot_own), (mix, mix_own),
            )
        )
    ]
    for copy in loads:
        copy.start()

    chip_y, core = la // 4, lax.rem(la, 2)
    chip_x, chip_z = 2 * lax.rem(la // 2, 2) + lo // 8, lax.rem(lo, 8)
    plane_rank, line_rank = 4 * chip_y + chip_x, 8 * core + chip_z

    def plane(step):
        y, x = lax.rem(chip_y + step[0], 4), lax.rem(chip_x + step[1], 4)
        return 4 * y + x, (4 * y + 2 * (x // 2) + core, 8 * lax.rem(x, 2) + chip_z)

    def line_of(step):
        other, z = lax.rem(core + step[0], 2), lax.rem(chip_z + step[1], 8)
        return 8 * other + z, (la - core + other, lo - chip_z + z)

    barrier = pltpu.get_barrier_semaphore()

    def greet(dev_lat, dev_lon):
        pl.semaphore_signal(
            barrier, inc=1, device_id=(dev_lat, dev_lon), device_id_type=MESH
        )

    for dev_lat in (up, down):
        for dev_lon in (left, right):
            greet(dev_lat, dev_lon)

    greet(la, left)
    greet(la, right)
    greet(up, lo)
    greet(down, lo)
    for step in PLANE:
        greet(*plane(step)[1])
    for step in LINE:
        greet(*line_of(step)[1])

    def remote(src, dst, send, recv, dev_lat, dev_lon):
        return pltpu.make_async_remote_copy(
            src_ref=src, dst_ref=dst, send_sem=send, recv_sem=recv,
            device_id=(dev_lat, dev_lon), device_id_type=MESH,
        )

    edge = pl.ds(0, PADC)
    head, tail = pl.ds(0, 16), pl.ds(32, 16)
    halo_plan = (
        (feat.at[pl.ds(0, REACH)], from_right, la, left),
        (feat.at[pl.ds(COLS - REACH, REACH)], from_left, la, right),
        (marks, marks_right, la, left),
        (marks, marks_left, la, right),
        (mask_own.at[0], mark_bottom, up, lo),
        (mask_own.at[ROWS - 1], mark_top, down, lo),
        (marks, marks_corner.at[0], up, left),
        (marks, marks_corner.at[1], up, right),
        (marks, marks_corner.at[2], down, left),
        (marks, marks_corner.at[3], down, right),
        (field.at[1, edge], field.at[ROWS + 1, edge], up, lo),
        (field.at[ROWS, edge], field.at[0, edge], down, lo),
        (field.at[1, head], corners.at[0], up, left),
        (field.at[1, tail], corners.at[1], up, right),
        (field.at[ROWS, head], corners.at[2], down, left),
        (field.at[ROWS, tail], corners.at[3], down, right),
    )
    halos = [
        remote(src, dst, halo_send.at[n], halo_recv.at[n], dev_lat, dev_lon)
        for n, (src, dst, dev_lat, dev_lon) in enumerate(halo_plan)
    ]

    pl.semaphore_wait(barrier, 8 + len(PLANE) + len(LINE))
    for copy in halos[0:2]:
        copy.start()

    loads[0].wait()
    flags = mask_own[...].reshape(ROWS * GROUPS, COLS).astype(F32).T.astype(BF16)
    row, col = iota((16, COLS), 0), iota((16, COLS), 1)
    pick = one_hot(col == jnp.where(row < 8, row, row + COLS - 16))
    marks[...] = dot(pick, flags).astype(BF16)
    for copy in halos[2:10]:
        copy.start()

    def widen(ref, n, rows):
        where = pl.ds(pl.multiple_of(ROWS * n, 8), ROWS)
        rows = rows.astype(F32)
        ref[0, where] = rows[:, 0:128]
        ref[1, where] = rows[:, 128:256]

    def cycle_of(ref, i, count):
        where = pl.ds(i, count, stride=ROWS)
        return jnp.concatenate([ref[0, where], ref[1, where]], axis=1)

    loads[1].wait()

    @pl.loop(0, COLS, unroll=5)
    def _(n):
        widen(wide_feat, n, feat_own[n])

    def spread(values, i):
        n, k = divmod(i, 16)
        part = values[:, 128 * n : min(128 * n + 128, ROWS * GROUPS)]
        depth = part.shape[1]
        table = one_hot(
            iota((depth, CHAN), 0) == iota((depth, CHAN), 1) // WIDTH + GROUPS * k
        )
        return dot(part, table)

    order = [0, ROWS - 1] + list(range(1, ROWS - 1))
    for i in order:
        wide = spread(flags, i)
        field[i + 1, 0:PADC] = pad_rows(
            cycle_of(wide_feat, i, COLS) * wide
        ).astype(BF16)
        seen[i + 1, 0:PADC] = pad_rows(wide).astype(BF16)
        if i == ROWS - 1:
            for copy in halos[10:]:
                copy.start()

    loads[2].wait()
    cycle = iota((BASES, n_lat * ROWS), 1)
    for a in range(3):
        outside = {0: cycle == 0, 1: cycle < 0, 2: cycle == n_lat * ROWS - 1}[a]
        for e in range(TAPS):
            first = BASES * (TAPS * a + e)
            tap_rows[first : first + BASES] = jnp.where(
                outside, 0.0, taps_own[a, e].astype(F32)
            )
    tap_rows[BASES * 3 * TAPS :] = jnp.zeros((8 - BASES * 3 * TAPS % 8, n_lat * ROWS), F32)
    shape = (ROWS, n_lat * ROWS)
    choose = one_hot(iota(shape, 1) == iota(shape, 0) + la * ROWS)
    mine = lax.dot_general(
        choose, tap_rows[...].astype(BF16), (((1,), (1,)), ((), ())), preferred_element_type=F32
    ).astype(BF16)
    shape = (mine.shape[1], CHAN)
    slot, entry = iota(shape, 1) // SLOT, iota(shape, 1) % SLOT
    odd = iota((ROWS, CHAN), 0) % 2 == 1
    away = jnp.abs(iota((1, CHAN), 1) % SLOT - REACH)
    for b in range(BASES):
        home = (entry < TAPS) & (slot < 3) & (
            iota(shape, 0) == BASES * (TAPS * slot + entry) + b
        )
        line = dot(mine, one_hot(home))
        line = jnp.where(odd, pltpu.roll(line, SLOT, 1), line)
        for i in range(ROWS):
            base[i, b : b + 1] = jnp.where(
                away <= width[la * ROWS + i], line[i : i + 1], 0.0
            )

    lane = iota((PADC, 128), 1) % SLOT

    @pl.loop(0, PAIRS, unroll=2)
    def _(t):
        for k in range(2):
            for b in range(BASES):
                for v in range(2):
                    line = base[2 * t + k, b : b + 1, v * 128 : v * 128 + 128]
                    row = jnp.broadcast_to(line, (PADC, 128))
                    late = pltpu.roll(jnp.broadcast_to(line, (8, 128)), 3, 1)
                    late = jnp.concatenate([late, late], axis=0)
                    own = pltpu.roll(row, 120, 1, stride=1, stride_axis=0)
                    high = pltpu.roll(late, 24, 1, stride=1, stride_axis=0)
                    low = pltpu.roll(row[0:8], 56, 1, stride=1, stride_axis=0)
                    piece = jnp.concatenate(
                        [
                            jnp.where(
                                lane[0:8] < COLS, own[0:8], jnp.where(lane[0:8] < 56, 0.0, low)
                            ),
                            own[8:32],
                            jnp.where(
                                lane[0:16] < COLS,
                                own[32:48],
                                jnp.where(
                                    (lane[0:16] >= PADC) & (lane[0:16] < 56), high, 0.0
                                ),
                            ),
                        ],
                        axis=0,
                    )
                    start = (k * BASES + b) * PADC
                    band[t, start : start + PADC, v * 128 : v * 128 + 128] = piece.astype(BF16)

    loads[3].wait()

    @pl.loop(0, COLS, unroll=5)
    def _(n):
        widen(wide_cot, n, cot_own[n])

    for i in range(ROWS):
        cots[i * PADC : i * PADC + PADC] = pad_rows(
            cycle_of(wide_cot, i, COLS)
        ).astype(BF16)
    for n in range(ROWS * PADC // 128):
        cots_t[:, n * 128 : n * 128 + 128] = cots[n * 128 : n * 128 + 128].T

    for copy in halos[2:]:
        copy.wait_recv()
    upper = iota((16, ROWS * GROUPS), 0) < 8

    def merged(high, low):
        return jnp.where(upper, high.astype(F32), low.astype(F32)).astype(BF16)

    both = merged(marks_right[...], marks_left[...])
    one_row = one_hot(iota((GROUPS, CHAN), 1) // WIDTH == iota((GROUPS, CHAN), 0))
    for i, ref, cycle, high, low in (
        (0, mark_top, ROWS - 1, 2, 3), (ROWS + 1, mark_bottom, 0, 0, 1)
    ):
        flat = dot(ref[...].astype(F32).T.astype(BF16), one_row)
        seen[i, 0:PADC] = pad_rows(flat).astype(BF16)
        pair = merged(marks_corner[high], marks_corner[low])
        seen[i, PADC:SLOT] = spread(pair, cycle).astype(BF16)
        ends = pltpu.roll(corners[low].astype(F32), 11, 0)
        field[i, PADC:SLOT] = jnp.concatenate(
            [corners[high].astype(F32)[0:8], ends[0:8]], axis=0
        ).astype(BF16)
    for copy in halos[0:2]:
        copy.wait_recv()

    @pl.loop(0, REACH, unroll=4)
    def _(n):
        widen(wide_feat, n, from_right[n])
        widen(wide_feat, n + REACH, from_left[n])

    for i in range(ROWS):
        wide = spread(both, i)
        field[i + 1, PADC:SLOT] = (
            cycle_of(wide_feat, i, 2 * REACH) * wide
        ).astype(BF16)
        seen[i + 1, PADC:SLOT] = wide.astype(BF16)

    @pl.loop(0, PAIRS, unroll=2)
    def _(t):
        weights = band[t]
        numerator = dot(weights, field[pl.ds(2 * t, 4)].reshape(4 * SLOT, CHAN))
        denominator = dot(weights, seen[pl.ds(2 * t, 4)].reshape(4 * SLOT, CHAN))
        shrink = 1.0 / jnp.maximum(denominator, 1.0)
        normal = (numerator * shrink).astype(BF16)
        for k in range(2):
            start = pl.multiple_of((2 * t + k) * PADC, PADC)
            for b in range(BASES):
                first = (k * BASES + b) * PADC
                scaled[b, pl.ds(start, PADC)] = normal[first : first + PADC]
        inverse[t] = shrink

    block = iota((CHAN, CHAN), 0) // WIDTH == iota((CHAN, CHAN), 1) // WIDTH
    for b in range(BASES):
        grad = jnp.where(block, dot(cots_t[...], scaled[b]), 0.0)
        share[b * WIDTH : b * WIDTH + WIDTH] = jnp.sum(grad.reshape(GROUPS, WIDTH, CHAN), axis=0)

    def gather_share(n):
        to, device = plane(PLANE[n])
        rows = pl.ds(pl.multiple_of(to * 8, 8), 8)
        return remote(
            share.at[rows], got_plane.at[n], sum_send.at[0, n], sum_recv.at[0, n], *device
        )

    def swap_share(n):
        _, device = line_of(LINE[n])
        here = got_line.at[line_rank]
        return remote(here, here, sum_send.at[1, n], sum_recv.at[1, n], *device)

    def spread_share(n):
        _, device = plane(PLANE[n])
        here = final.at[plane_rank]
        return remote(here, here, sum_send.at[2, n], sum_recv.at[2, n], *device)

    def start_all(make):
        copies = [make(n) for n in range(15)]
        for copy in copies:
            copy.start()
        return copies

    def finish_all(copies):
        for copy in copies:
            copy.wait_recv()

    gathers = start_all(gather_share)

    loads[4].wait()
    repeat = one_hot(iota((WIDTH, CHAN), 1) % WIDTH == iota((WIDTH, CHAN), 0))
    for b in range(BASES):
        tall = mix_own[:, b].reshape(CHAN, WIDTH)
        mixer[b] = jnp.where(block, dot(tall, repeat), 0.0).astype(BF16)

    @pl.loop(0, PAIRS // 4)
    def _(n):
        start = pl.multiple_of(n * 8 * PADC, 8 * PADC)
        rows = cots[pl.ds(start, 8 * PADC)]
        for b in range(BASES):
            result = lax.dot_general(
                rows, mixer[b], (((1,), (1,)), ((), ())), preferred_element_type=F32
            )
            for i in range(8):
                first = ((i % 2) * BASES + b) * PADC
                here = 4 * n + i // 2
                pulled[here, first : first + PADC] = (
                    result[i * PADC : i * PADC + PADC] * inverse[here, first : first + PADC]
                ).astype(BF16)

    total[0:2] = jnp.zeros((2, SLOT, CHAN), F32)

    @pl.loop(0, PAIRS, unroll=2)
    def _(t):
        result = dot(band[t].T, pulled[t]).reshape(4, SLOT, CHAN)
        total[pl.ds(2 * t, 2)] += result[0:2]
        total[pl.ds(2 * t + 2, 2)] = result[2:4]

    inner = pl.ds(1, ROWS)
    high, low, own = pl.ds(PADC, 8), pl.ds(56, 8), pl.ds(0, PADC)
    part_plan = (
        (total.at[inner, low], part_right, la, left),
        (total.at[inner, high], part_left, la, right),
        (total.at[0, own], part_bottom, up, lo),
        (total.at[ROWS + 1, own], part_top, down, lo),
        (total.at[0, low], part_corner.at[0], up, left),
        (total.at[0, high], part_corner.at[1], up, right),
        (total.at[ROWS + 1, low], part_corner.at[2], down, left),
        (total.at[ROWS + 1, high], part_corner.at[3], down, right),
    )
    parts = [
        remote(src, dst, part_send.at[n], part_recv.at[n], dev_lat, dev_lon)
        for n, (src, dst, dev_lat, dev_lon) in enumerate(part_plan)
    ]
    for copy in parts:
        copy.start()

    finish_all(gathers)
    got_line[line_rank] = share[pl.ds(pl.multiple_of(plane_rank * 8, 8), 8)] + jnp.sum(
        got_plane[...], axis=0
    )
    swaps = start_all(swap_share)

    def spill(ref, i, rows):
        where = pl.ds(i, COLS, stride=ROWS)
        ref[0, where] = rows[0:COLS, 0:128]
        ref[1, where] = rows[0:COLS, 128:256]

    def narrow(ref, out):
        @pl.loop(0, COLS, unroll=5)
        def _(n):
            where = pl.ds(pl.multiple_of(ROWS * n, 8), ROWS)
            out[n] = jnp.concatenate([ref[0, where], ref[1, where]], axis=1).astype(BF16)

    @pl.loop(0, PAIRS // 4)
    def _(n):
        start = pl.multiple_of(n * 8 * PADC, 8 * PADC)
        result = dot(scaled[0, pl.ds(start, 8 * PADC)], mixer[0])
        for b in range(1, BASES):
            result += dot(scaled[b, pl.ds(start, 8 * PADC)], mixer[b])
        for i in range(8):
            spill(wide_cot, 8 * n + i, result[i * PADC : i * PADC + PADC])

    narrow(wide_cot, cot_own)
    stores = [pltpu.make_async_copy(cot_own, infilled, store_sem.at[0])]
    stores[0].start()

    finish_all(swaps)
    final[plane_rank] = jnp.sum(got_line[...], axis=0) * (
        1.0 / math.sqrt(ROWS * n_lat * COLS * n_lon)
    )
    spreads = start_all(spread_share)

    for copy in parts:
        copy.wait_recv()
    for copy in parts:
        copy.wait_send()

    part_left[0] += part_corner[3]
    part_right[0] += part_corner[2]
    part_left[ROWS - 1] += part_corner[1]
    part_right[ROWS - 1] += part_corner[0]
    total[1, 0:PADC] += part_top[...]
    total[ROWS, 0:PADC] += part_bottom[...]

    @pl.loop(0, ROWS, unroll=2)
    def _(i):
        after = pltpu.roll(
            jnp.concatenate([part_right[i], jnp.zeros((8, CHAN), F32)], axis=0), 5, 0
        )
        extra = jnp.concatenate([part_left[i], jnp.zeros((24, CHAN), F32), after], axis=0)
        result = (total[i + 1, 0:PADC] + extra) * seen[i + 1, 0:PADC].astype(F32)
        spill(wide_feat, i, result)

    narrow(wide_feat, feat_own)
    stores.append(pltpu.make_async_copy(feat_own, input_grad, store_sem.at[1]))
    stores[1].start()
    for copy in halos:
        copy.wait_send()

    for copy in gathers + swaps:
        copy.wait_send()

    finish_all(spreads)
    for copy in spreads:
        copy.wait_send()
    stores.append(pltpu.make_async_copy(final, weight_sum, store_sem.at[2]))
    stores[2].start()
    for copy in stores:
        copy.wait()


def finish(
    sums, first, second, grads, first_out, second_out, held, sums_own, grads_own, in_sem, out_sem
):
    load_sums = pltpu.make_async_copy(sums, sums_own, in_sem.at[6])
    load_sums.start()
    step = COLS // 3
    loads, stores = [], []
    for n, (src, dst) in enumerate(((first, first_out), (second, second_out))):
        for k in range(3):
            part = pl.ds(k * step, step)
            loads.append(
                pltpu.make_async_copy(src.at[part], held.at[n, part], in_sem.at[3 * n + k])
            )
            stores.append(
                pltpu.make_async_copy(held.at[n, part], dst.at[part], out_sem.at[3 * n + k])
            )
    for copy in loads:
        copy.start()
    load_sums.wait()
    for b in range(BASES):
        grad = sums_own[4 * b : 4 * b + 4].reshape(WIDTH, CHAN)
        grads_own[:, b] = grad.T.reshape(GROUPS, WIDTH, WIDTH)
    stores.append(pltpu.make_async_copy(grads_own, grads, out_sem.at[6]))
    stores[6].start()
    for load, store in zip(loads, stores):
        load.wait()
        store.start()
    for copy in stores:
        copy.wait()


def local(features, obs_mask, filter_taps, band_width, mixing, cotangent):
    n_lat, n_lon = lax.axis_size("lat"), lax.axis_size("lon")
    anywhere = pl.BlockSpec(memory_space=pltpu.HBM)
    marks = pltpu.VMEM((16, ROWS * GROUPS), BF16)
    field = jax.ShapeDtypeStruct((COLS, ROWS, CHAN), BF16)
    infilled, input_grad, sums = pl.pallas_call(
        functools.partial(kernel, n_lat, n_lon),
        out_shape=(
            field,
            field,
            jax.ShapeDtypeStruct((n_lon, 8, CHAN), F32),
        ),
        in_specs=[anywhere] * 3 + [pl.BlockSpec(memory_space=pltpu.SMEM)] + [anywhere] * 2,
        out_specs=(anywhere,) * 3,
        scratch_shapes=[
            pltpu.VMEM((COLS, ROWS, CHAN), BF16),
            pltpu.VMEM((ROWS, GROUPS, COLS), jnp.int32),
            pltpu.VMEM((3, TAPS, BASES, n_lat * ROWS), BF16),
            pltpu.VMEM((GROUPS, BASES, WIDTH, WIDTH), BF16),
            pltpu.VMEM((COLS, ROWS, CHAN), BF16),
            pltpu.VMEM((2, COLS * ROWS, 128), F32),
            pltpu.VMEM((2, COLS * ROWS, 128), F32),
            pltpu.VMEM((208, n_lat * ROWS), F32),
            pltpu.VMEM((ROWS, BASES, CHAN), F32),
            pltpu.VMEM((ROWS + 2, SLOT, CHAN), BF16),
            pltpu.VMEM((ROWS + 2, SLOT, CHAN), BF16),
            pltpu.VMEM((ROWS * PADC, CHAN), BF16),
            pltpu.VMEM((CHAN, ROWS * PADC), BF16),
            pltpu.VMEM((BASES, CHAN, CHAN), BF16),
            pltpu.VMEM((PAIRS, BAND, 4 * SLOT), BF16),
            pltpu.VMEM((BASES, ROWS * PADC, CHAN), BF16),
            pltpu.VMEM((PAIRS, BAND, CHAN), BF16),
            pltpu.VMEM((PAIRS, BAND, CHAN), F32),
            pltpu.VMEM((ROWS + 2, SLOT, CHAN), F32),
            pltpu.VMEM((REACH, ROWS, CHAN), BF16),
            pltpu.VMEM((REACH, ROWS, CHAN), BF16),
            marks, marks, marks,
            pltpu.VMEM((4, 16, ROWS * GROUPS), BF16),
            pltpu.VMEM((GROUPS, COLS), jnp.int32),
            pltpu.VMEM((GROUPS, COLS), jnp.int32),
            pltpu.VMEM((4, 16, CHAN), BF16),
            pltpu.VMEM((BASES * WIDTH, CHAN), F32),
            pltpu.VMEM((15, 8, CHAN), F32),
            pltpu.VMEM((16, 8, CHAN), F32),
            pltpu.VMEM((16, 8, CHAN), F32),
            pltpu.VMEM((ROWS, 8, CHAN), F32),
            pltpu.VMEM((ROWS, 8, CHAN), F32),
            pltpu.VMEM((PADC, CHAN), F32),
            pltpu.VMEM((PADC, CHAN), F32),
            pltpu.VMEM((4, 8, CHAN), F32),
            pltpu.SemaphoreType.DMA((5,)),
            pltpu.SemaphoreType.DMA((3,)),
            pltpu.SemaphoreType.DMA((16,)),
            pltpu.SemaphoreType.DMA((16,)),
            pltpu.SemaphoreType.DMA((8,)),
            pltpu.SemaphoreType.DMA((8,)),
            pltpu.SemaphoreType.DMA((3, 16)),
            pltpu.SemaphoreType.DMA((3, 16)),
        ],
        compiler_params=pltpu.CompilerParams(
            collective_id=0, has_side_effects=True, vmem_limit_bytes=56 * 1024 * 1024
        ),
    )(
        features.transpose(1, 0, 2),
        obs_mask.transpose(0, 2, 1),
        filter_taps.transpose(2, 3, 1, 0),
        band_width,
        mixing,
        cotangent.transpose(1, 0, 2),
    )
    weight_grad, infilled, input_grad = pl.pallas_call(
        finish,
        out_shape=(jax.ShapeDtypeStruct((GROUPS, BASES, WIDTH, WIDTH), F32), field, field),
        in_specs=[anywhere] * 3,
        out_specs=(anywhere,) * 3,
        scratch_shapes=[
            pltpu.VMEM((2, COLS, ROWS, CHAN), BF16),
            pltpu.VMEM((n_lon, 8, CHAN), F32),
            pltpu.VMEM((GROUPS, BASES, WIDTH, WIDTH), F32),
            pltpu.SemaphoreType.DMA((7,)),
            pltpu.SemaphoreType.DMA((7,)),
        ],
        compiler_params=pltpu.CompilerParams(vmem_limit_bytes=56 * 1024 * 1024),
    )(sums, infilled, input_grad)
    return infilled.transpose(1, 0, 2), input_grad.transpose(1, 0, 2), weight_grad


def solution(mesh):
    placed = (P("lat", "lon", None), P("lat", "lon", None), P(), P(), P(), P("lat", "lon", None))
    return jax.shard_map(
        local,
        mesh=mesh,
        in_specs=placed,
        out_specs=(P("lat", "lon", None), P("lat", "lon", None), P()),
        check_vma=False,
    )
```

```python
import functools
import math

import jax
import jax.numpy as jnp
from jax import lax
from jax.experimental import pallas as pl
from jax.experimental.pallas import tpu as pltpu
from jax.sharding import PartitionSpec as P

MESH = pl.DeviceIdType.MESH
F32 = jnp.float32
BF16 = jnp.bfloat16
ROWS = 24
COLS = 45
PADC = 48
SLOT = 64
CHAN = 256
GROUPS = 8
WIDTH = 32
BASES = 4
REACH = 8
TAPS = 2 * REACH + 1
PAIRS = ROWS // 2
BAND = 2 * BASES * PADC


def far_first(sizes):
    steps = [(a, b) for a in range(sizes[0]) for b in range(sizes[1])]
    hops = lambda s: sum(min(k, n - k) for k, n in zip(s, sizes))
    return sorted(steps, key=lambda s: (-hops(s), s))[:-1]


PLANE = far_first((4, 4))
LINE = far_first((2, 8))


def iota(shape, dim):
    return lax.broadcasted_iota(jnp.int32, shape, dim)


def one_hot(test):
    return jnp.where(test, 1.0, 0.0).astype(BF16)


def dot(a, b):
    return jnp.dot(a, b, preferred_element_type=F32)


def pad_rows(x):
    return jnp.concatenate([x, jnp.zeros((PADC - COLS, x.shape[1]), F32)], axis=0)


def kernel(
    n_lat, n_lon,
    feat, mask, taps, width, mix, cot,
    infilled, input_grad, weight_sum,
    feat_own, mask_own, taps_own, mix_own, cot_own,
    wide_feat, wide_cot, tap_rows, base,
    field, seen, cots, cots_t, mixer, band, scaled, pulled, back, total,
    from_right, from_left, marks, marks_right, marks_left, marks_corner, mark_top, mark_bottom,
    corners, share, got_plane, got_line, final,
    part_right, part_left, part_top, part_bottom, part_corner,
    load_sem, store_sem, halo_send, halo_recv, part_send, part_recv, sum_send, sum_recv,
):
    la, lo = lax.axis_index("lat"), lax.axis_index("lon")
    up, down = lax.rem(la + n_lat - 1, n_lat), lax.rem(la + 1, n_lat)
    left, right = lax.rem(lo + n_lon - 1, n_lon), lax.rem(lo + 1, n_lon)

    loads = [
        pltpu.make_async_copy(src, dst, load_sem.at[n])
        for n, (src, dst) in enumerate(
            (
                (mask, mask_own), (feat, feat_own), (taps, taps_own),
                (cot, cot_own), (mix, mix_own),
            )
        )
    ]
    for copy in loads:
        copy.start()

    chip_y, core = la // 4, lax.rem(la, 2)
    chip_x, chip_z = 2 * lax.rem(la // 2, 2) + lo // 8, lax.rem(lo, 8)
    plane_rank, line_rank = 4 * chip_y + chip_x, 8 * core + chip_z

    def plane(step):
        y, x = lax.rem(chip_y + step[0], 4), lax.rem(chip_x + step[1], 4)
        return 4 * y + x, (4 * y + 2 * (x // 2) + core, 8 * lax.rem(x, 2) + chip_z)

    def line_of(step):
        other, z = lax.rem(core + step[0], 2), lax.rem(chip_z + step[1], 8)
        return 8 * other + z, (la - core + other, lo - chip_z + z)

    barrier = pltpu.get_barrier_semaphore()

    def greet(dev_lat, dev_lon):
        pl.semaphore_signal(
            barrier, inc=1, device_id=(dev_lat, dev_lon), device_id_type=MESH
        )

    for dev_lat in (up, down):
        for dev_lon in (left, right):
            greet(dev_lat, dev_lon)

    greet(la, left)
    greet(la, right)
    greet(up, lo)
    greet(down, lo)
    for step in PLANE:
        greet(*plane(step)[1])
    for step in LINE:
        greet(*line_of(step)[1])

    def remote(src, dst, send, recv, dev_lat, dev_lon):
        return pltpu.make_async_remote_copy(
            src_ref=src, dst_ref=dst, send_sem=send, recv_sem=recv,
            device_id=(dev_lat, dev_lon), device_id_type=MESH,
        )

    edge = pl.ds(0, PADC)
    head, tail = pl.ds(0, 16), pl.ds(32, 16)
    halo_plan = (
        (feat.at[pl.ds(0, REACH)], from_right, la, left),
        (feat.at[pl.ds(COLS - REACH, REACH)], from_left, la, right),
        (marks, marks_right, la, left),
        (marks, marks_left, la, right),
        (mask_own.at[0], mark_bottom, up, lo),
        (mask_own.at[ROWS - 1], mark_top, down, lo),
        (marks, marks_corner.at[0], up, left),
        (marks, marks_corner.at[1], up, right),
        (marks, marks_corner.at[2], down, left),
        (marks, marks_corner.at[3], down, right),
        (field.at[1, edge], field.at[ROWS + 1, edge], up, lo),
        (field.at[ROWS, edge], field.at[0, edge], down, lo),
        (field.at[1, head], corners.at[0], up, left),
        (field.at[1, tail], corners.at[1], up, right),
        (field.at[ROWS, head], corners.at[2], down, left),
        (field.at[ROWS, tail], corners.at[3], down, right),
    )
    halos = [
        remote(src, dst, halo_send.at[n], halo_recv.at[n], dev_lat, dev_lon)
        for n, (src, dst, dev_lat, dev_lon) in enumerate(halo_plan)
    ]

    pl.semaphore_wait(barrier, 8 + len(PLANE) + len(LINE))
    for copy in halos[0:2]:
        copy.start()

    loads[0].wait()
    flags = mask_own[...].reshape(ROWS * GROUPS, COLS).astype(F32).T.astype(BF16)
    row, col = iota((16, COLS), 0), iota((16, COLS), 1)
    pick = one_hot(col == jnp.where(row < 8, row, row + COLS - 16))
    marks[...] = dot(pick, flags).astype(BF16)
    for copy in halos[2:10]:
        copy.start()

    def widen(ref, n, rows):
        where = pl.ds(pl.multiple_of(ROWS * n, 8), ROWS)
        rows = rows.astype(F32)
        ref[0, where] = rows[:, 0:128]
        ref[1, where] = rows[:, 128:256]

    def cycle_of(ref, i, count):
        where = pl.ds(i, count, stride=ROWS)
        return jnp.concatenate([ref[0, where], ref[1, where]], axis=1)

    loads[1].wait()

    @pl.loop(0, COLS, unroll=5)
    def _(n):
        widen(wide_feat, n, feat_own[n])

    def spread(values, i):
        n, k = divmod(i, 16)
        part = values[:, 128 * n : min(128 * n + 128, ROWS * GROUPS)]
        depth = part.shape[1]
        table = one_hot(
            iota((depth, CHAN), 0) == iota((depth, CHAN), 1) // WIDTH + GROUPS * k
        )
        return dot(part, table)

    order = [0, ROWS - 1] + list(range(1, ROWS - 1))
    for i in order:
        wide = spread(flags, i)
        field[i + 1, 0:PADC] = pad_rows(
            cycle_of(wide_feat, i, COLS) * wide
        ).astype(BF16)
        seen[i + 1, 0:PADC] = pad_rows(wide).astype(BF16)
        if i == ROWS - 1:
            for copy in halos[10:]:
                copy.start()

    loads[2].wait()
    cycle = iota((BASES, n_lat * ROWS), 1)
    for a in range(3):
        outside = {0: cycle == 0, 1: cycle < 0, 2: cycle == n_lat * ROWS - 1}[a]
        for e in range(TAPS):
            first = BASES * (TAPS * a + e)
            tap_rows[first : first + BASES] = jnp.where(
                outside, 0.0, taps_own[a, e].astype(F32)
            )
    tap_rows[BASES * 3 * TAPS :] = jnp.zeros((8 - BASES * 3 * TAPS % 8, n_lat * ROWS), F32)
    shape = (ROWS, n_lat * ROWS)
    choose = one_hot(iota(shape, 1) == iota(shape, 0) + la * ROWS)
    mine = lax.dot_general(
        choose, tap_rows[...].astype(BF16), (((1,), (1,)), ((), ())), preferred_element_type=F32
    ).astype(BF16)
    shape = (mine.shape[1], CHAN)
    slot, entry = iota(shape, 1) // SLOT, iota(shape, 1) % SLOT
    odd = iota((ROWS, CHAN), 0) % 2 == 1
    away = jnp.abs(iota((1, CHAN), 1) % SLOT - REACH)
    for b in range(BASES):
        home = (entry < TAPS) & (slot < 3) & (
            iota(shape, 0) == BASES * (TAPS * slot + entry) + b
        )
        line = dot(mine, one_hot(home))
        line = jnp.where(odd, pltpu.roll(line, SLOT, 1), line)
        for i in range(ROWS):
            base[i, b : b + 1] = jnp.where(
                away <= width[la * ROWS + i], line[i : i + 1], 0.0
            )

    lane = iota((PADC, 128), 1) % SLOT

    @pl.loop(0, PAIRS)
    def _(t):
        for k in range(2):
            for b in range(BASES):
                for v in range(2):
                    line = base[2 * t + k, b : b + 1, v * 128 : v * 128 + 128]
                    row = jnp.broadcast_to(line, (PADC, 128))
                    late = pltpu.roll(jnp.broadcast_to(line, (8, 128)), 3, 1)
                    late = jnp.concatenate([late, late], axis=0)
                    own = pltpu.roll(row, 120, 1, stride=1, stride_axis=0)
                    high = pltpu.roll(late, 24, 1, stride=1, stride_axis=0)
                    low = pltpu.roll(row[0:8], 56, 1, stride=1, stride_axis=0)
                    piece = jnp.concatenate(
                        [
                            jnp.where(
                                lane[0:8] < COLS, own[0:8], jnp.where(lane[0:8] < 56, 0.0, low)
                            ),
                            own[8:32],
                            jnp.where(
                                lane[0:16] < COLS,
                                own[32:48],
                                jnp.where(
                                    (lane[0:16] >= PADC) & (lane[0:16] < 56), high, 0.0
                                ),
                            ),
                        ],
                        axis=0,
                    )
                    start = (k * BASES + b) * PADC
                    band[t, start : start + PADC, v * 128 : v * 128 + 128] = piece.astype(BF16)

    loads[3].wait()

    @pl.loop(0, COLS, unroll=5)
    def _(n):
        widen(wide_cot, n, cot_own[n])

    for i in range(ROWS):
        cots[i * PADC : i * PADC + PADC] = pad_rows(
            cycle_of(wide_cot, i, COLS)
        ).astype(BF16)
    for n in range(ROWS * PADC // 128):
        cots_t[:, n * 128 : n * 128 + 128] = cots[n * 128 : n * 128 + 128].T

    loads[4].wait()
    block = iota((CHAN, CHAN), 0) // WIDTH == iota((CHAN, CHAN), 1) // WIDTH
    repeat = one_hot(iota((WIDTH, CHAN), 1) % WIDTH == iota((WIDTH, CHAN), 0))
    for b in range(BASES):
        tall = mix_own[:, b].reshape(CHAN, WIDTH)
        mixer[b] = jnp.where(block, dot(tall, repeat), 0.0).astype(BF16)

    @pl.loop(0, PAIRS // 4)
    def _(n):
        start = pl.multiple_of(n * 8 * PADC, 8 * PADC)
        rows = cots[pl.ds(start, 8 * PADC)]
        for b in range(BASES):
            result = lax.dot_general(
                rows, mixer[b], (((1,), (1,)), ((), ())), preferred_element_type=F32
            )
            for i in range(8):
                first = ((i % 2) * BASES + b) * PADC
                back[4 * n + i // 2, first : first + PADC] = result[i * PADC : i * PADC + PADC]

    for copy in halos[2:]:
        copy.wait_recv()
    upper = iota((16, ROWS * GROUPS), 0) < 8

    def merged(high, low):
        return jnp.where(upper, high.astype(F32), low.astype(F32)).astype(BF16)

    both = merged(marks_right[...], marks_left[...])
    one_row = one_hot(iota((GROUPS, CHAN), 1) // WIDTH == iota((GROUPS, CHAN), 0))
    for i, ref, cycle, high, low in (
        (0, mark_top, ROWS - 1, 2, 3), (ROWS + 1, mark_bottom, 0, 0, 1)
    ):
        flat = dot(ref[...].astype(F32).T.astype(BF16), one_row)
        seen[i, 0:PADC] = pad_rows(flat).astype(BF16)
        pair = merged(marks_corner[high], marks_corner[low])
        seen[i, PADC:SLOT] = spread(pair, cycle).astype(BF16)
        ends = pltpu.roll(corners[low].astype(F32), 11, 0)
        field[i, PADC:SLOT] = jnp.concatenate(
            [corners[high].astype(F32)[0:8], ends[0:8]], axis=0
        ).astype(BF16)
    for copy in halos[0:2]:
        copy.wait_recv()

    @pl.loop(0, REACH, unroll=4)
    def _(n):
        widen(wide_feat, n, from_right[n])
        widen(wide_feat, n + REACH, from_left[n])

    for i in range(ROWS):
        wide = spread(both, i)
        field[i + 1, PADC:SLOT] = (
            cycle_of(wide_feat, i, 2 * REACH) * wide
        ).astype(BF16)
        seen[i + 1, PADC:SLOT] = wide.astype(BF16)

    @pl.loop(0, PAIRS, unroll=4)
    def _(t):
        weights = band[t]
        numerator = dot(weights, field[pl.ds(2 * t, 4)].reshape(4 * SLOT, CHAN))
        denominator = dot(weights, seen[pl.ds(2 * t, 4)].reshape(4 * SLOT, CHAN))
        shrink = 1.0 / jnp.maximum(denominator, 1.0)
        normal = (numerator * shrink).astype(BF16)
        for k in range(2):
            start = pl.multiple_of((2 * t + k) * PADC, PADC)
            for b in range(BASES):
                first = (k * BASES + b) * PADC
                scaled[b, pl.ds(start, PADC)] = normal[first : first + PADC]
        pulled[t] = (back[t] * shrink).astype(BF16)

    for b in range(BASES):
        grad = jnp.where(block, dot(cots_t[...], scaled[b]), 0.0)
        share[b * WIDTH : b * WIDTH + WIDTH] = jnp.sum(grad.reshape(GROUPS, WIDTH, CHAN), axis=0)

    def gather_share(n):
        to, device = plane(PLANE[n])
        rows = pl.ds(pl.multiple_of(to * 8, 8), 8)
        return remote(
            share.at[rows], got_plane.at[n], sum_send.at[0, n], sum_recv.at[0, n], *device
        )

    def swap_share(n):
        _, device = line_of(LINE[n])
        here = got_line.at[line_rank]
        return remote(here, here, sum_send.at[1, n], sum_recv.at[1, n], *device)

    def spread_share(n):
        _, device = plane(PLANE[n])
        return remote(
            final, weight_sum.at[plane_rank], sum_send.at[2, n], sum_recv.at[2, n], *device
        )

    def start_all(make):
        copies = [make(n) for n in range(15)]
        for copy in copies:
            copy.start()
        return copies

    def finish_all(copies):
        for copy in copies:
            copy.wait_recv()

    gathers = start_all(gather_share)

    total[0:2] = jnp.zeros((2, SLOT, CHAN), F32)

    @pl.loop(0, PAIRS, unroll=4)
    def _(t):
        result = dot(band[t].T, pulled[t]).reshape(4, SLOT, CHAN)
        total[pl.ds(2 * t, 2)] += result[0:2]
        total[pl.ds(2 * t + 2, 2)] = result[2:4]

    inner = pl.ds(1, ROWS)
    high, low, own = pl.ds(PADC, 8), pl.ds(56, 8), pl.ds(0, PADC)
    part_plan = (
        (total.at[inner, low], part_right, la, left),
        (total.at[inner, high], part_left, la, right),
        (total.at[0, own], part_bottom, up, lo),
        (total.at[ROWS + 1, own], part_top, down, lo),
        (total.at[0, low], part_corner.at[0], up, left),
        (total.at[0, high], part_corner.at[1], up, right),
        (total.at[ROWS + 1, low], part_corner.at[2], down, left),
        (total.at[ROWS + 1, high], part_corner.at[3], down, right),
    )
    parts = [
        remote(src, dst, part_send.at[n], part_recv.at[n], dev_lat, dev_lon)
        for n, (src, dst, dev_lat, dev_lon) in enumerate(part_plan)
    ]
    for copy in parts:
        copy.start()

    finish_all(gathers)
    got_line[line_rank] = share[pl.ds(pl.multiple_of(plane_rank * 8, 8), 8)] + jnp.sum(
        got_plane[...], axis=0
    )
    swaps = start_all(swap_share)

    def spill(ref, i, rows):
        where = pl.ds(i, COLS, stride=ROWS)
        ref[0, where] = rows[0:COLS, 0:128]
        ref[1, where] = rows[0:COLS, 128:256]

    def narrow(ref, out):
        @pl.loop(0, COLS, unroll=5)
        def _(n):
            where = pl.ds(pl.multiple_of(ROWS * n, 8), ROWS)
            out[n] = jnp.concatenate([ref[0, where], ref[1, where]], axis=1).astype(BF16)

    @pl.loop(0, PAIRS // 4)
    def _(n):
        start = pl.multiple_of(n * 8 * PADC, 8 * PADC)
        result = dot(scaled[0, pl.ds(start, 8 * PADC)], mixer[0])
        for b in range(1, BASES):
            result += dot(scaled[b, pl.ds(start, 8 * PADC)], mixer[b])
        for i in range(8):
            spill(wide_cot, 8 * n + i, result[i * PADC : i * PADC + PADC])

    narrow(wide_cot, cot_own)
    stores = [pltpu.make_async_copy(cot_own, infilled, store_sem.at[0])]
    stores[0].start()

    finish_all(swaps)
    final[...] = jnp.sum(got_line[...], axis=0) * (
        1.0 / math.sqrt(ROWS * n_lat * COLS * n_lon)
    )
    spreads = start_all(spread_share)
    stores.append(pltpu.make_async_copy(final, weight_sum.at[plane_rank], store_sem.at[2]))
    stores[1].start()

    for copy in parts:
        copy.wait_recv()
    for copy in parts:
        copy.wait_send()

    part_left[0] += part_corner[3]
    part_right[0] += part_corner[2]
    part_left[ROWS - 1] += part_corner[1]
    part_right[ROWS - 1] += part_corner[0]
    total[1, 0:PADC] += part_top[...]
    total[ROWS, 0:PADC] += part_bottom[...]

    @pl.loop(0, ROWS, unroll=2)
    def _(i):
        after = pltpu.roll(
            jnp.concatenate([part_right[i], jnp.zeros((8, CHAN), F32)], axis=0), 5, 0
        )
        extra = jnp.concatenate([part_left[i], jnp.zeros((24, CHAN), F32), after], axis=0)
        result = (total[i + 1, 0:PADC] + extra) * seen[i + 1, 0:PADC].astype(F32)
        spill(wide_feat, i, result)

    narrow(wide_feat, feat_own)
    stores.append(pltpu.make_async_copy(feat_own, input_grad, store_sem.at[1]))
    stores[2].start()
    for copy in halos:
        copy.wait_send()

    for copy in gathers + swaps:
        copy.wait_send()

    finish_all(spreads)
    for copy in spreads:
        copy.wait_send()
    for copy in stores:
        copy.wait()


def finish(
    sums, first, second, grads, first_out, second_out, held, sums_own, grads_own, in_sem, out_sem
):
    load_sums = pltpu.make_async_copy(sums, sums_own, in_sem.at[6])
    load_sums.start()
    step = COLS // 3
    loads, stores = [], []
    for n, (src, dst) in enumerate(((first, first_out), (second, second_out))):
        for k in range(3):
            part = pl.ds(k * step, step)
            loads.append(
                pltpu.make_async_copy(src.at[part], held.at[n, part], in_sem.at[3 * n + k])
            )
            stores.append(
                pltpu.make_async_copy(held.at[n, part], dst.at[part], out_sem.at[3 * n + k])
            )
    for copy in loads:
        copy.start()
    load_sums.wait()
    for b in range(BASES):
        grad = sums_own[4 * b : 4 * b + 4].reshape(WIDTH, CHAN)
        grads_own[:, b] = grad.T.reshape(GROUPS, WIDTH, WIDTH)
    stores.append(pltpu.make_async_copy(grads_own, grads, out_sem.at[6]))
    stores[6].start()
    for load, store in zip(loads, stores):
        load.wait()
        store.start()
    for copy in stores:
        copy.wait()


def local(features, obs_mask, filter_taps, band_width, mixing, cotangent):
    n_lat, n_lon = lax.axis_size("lat"), lax.axis_size("lon")
    anywhere = pl.BlockSpec(memory_space=pltpu.HBM)
    marks = pltpu.VMEM((16, ROWS * GROUPS), BF16)
    field = jax.ShapeDtypeStruct((COLS, ROWS, CHAN), BF16)
    infilled, input_grad, sums = pl.pallas_call(
        functools.partial(kernel, n_lat, n_lon),
        out_shape=(
            field,
            field,
            jax.ShapeDtypeStruct((n_lon, 8, CHAN), F32),
        ),
        in_specs=[anywhere] * 3 + [pl.BlockSpec(memory_space=pltpu.SMEM)] + [anywhere] * 2,
        out_specs=(anywhere,) * 3,
        scratch_shapes=[
            pltpu.VMEM((COLS, ROWS, CHAN), BF16),
            pltpu.VMEM((ROWS, GROUPS, COLS), jnp.int32),
            pltpu.VMEM((3, TAPS, BASES, n_lat * ROWS), BF16),
            pltpu.VMEM((GROUPS, BASES, WIDTH, WIDTH), BF16),
            pltpu.VMEM((COLS, ROWS, CHAN), BF16),
            pltpu.VMEM((2, COLS * ROWS, 128), F32),
            pltpu.VMEM((2, COLS * ROWS, 128), F32),
            pltpu.VMEM((208, n_lat * ROWS), F32),
            pltpu.VMEM((ROWS, BASES, CHAN), F32),
            pltpu.VMEM((ROWS + 2, SLOT, CHAN), BF16),
            pltpu.VMEM((ROWS + 2, SLOT, CHAN), BF16),
            pltpu.VMEM((ROWS * PADC, CHAN), BF16),
            pltpu.VMEM((CHAN, ROWS * PADC), BF16),
            pltpu.VMEM((BASES, CHAN, CHAN), BF16),
            pltpu.VMEM((PAIRS, BAND, 4 * SLOT), BF16),
            pltpu.VMEM((BASES, ROWS * PADC, CHAN), BF16),
            pltpu.VMEM((PAIRS, BAND, CHAN), BF16),
            pltpu.VMEM((PAIRS, BAND, CHAN), F32),
            pltpu.VMEM((ROWS + 2, SLOT, CHAN), F32),
            pltpu.VMEM((REACH, ROWS, CHAN), BF16),
            pltpu.VMEM((REACH, ROWS, CHAN), BF16),
            marks, marks, marks,
            pltpu.VMEM((4, 16, ROWS * GROUPS), BF16),
            pltpu.VMEM((GROUPS, COLS), jnp.int32),
            pltpu.VMEM((GROUPS, COLS), jnp.int32),
            pltpu.VMEM((4, 16, CHAN), BF16),
            pltpu.VMEM((BASES * WIDTH, CHAN), F32),
            pltpu.VMEM((15, 8, CHAN), F32),
            pltpu.VMEM((16, 8, CHAN), F32),
            pltpu.VMEM((8, CHAN), F32),
            pltpu.VMEM((ROWS, 8, CHAN), F32),
            pltpu.VMEM((ROWS, 8, CHAN), F32),
            pltpu.VMEM((PADC, CHAN), F32),
            pltpu.VMEM((PADC, CHAN), F32),
            pltpu.VMEM((4, 8, CHAN), F32),
            pltpu.SemaphoreType.DMA((5,)),
            pltpu.SemaphoreType.DMA((3,)),
            pltpu.SemaphoreType.DMA((16,)),
            pltpu.SemaphoreType.DMA((16,)),
            pltpu.SemaphoreType.DMA((8,)),
            pltpu.SemaphoreType.DMA((8,)),
            pltpu.SemaphoreType.DMA((3, 16)),
            pltpu.SemaphoreType.DMA((3, 16)),
        ],
        compiler_params=pltpu.CompilerParams(
            collective_id=0, has_side_effects=True, vmem_limit_bytes=56 * 1024 * 1024
        ),
    )(
        features.transpose(1, 0, 2),
        obs_mask.transpose(0, 2, 1),
        filter_taps.transpose(2, 3, 1, 0),
        band_width,
        mixing,
        cotangent.transpose(1, 0, 2),
    )
    weight_grad, infilled, input_grad = pl.pallas_call(
        finish,
        out_shape=(jax.ShapeDtypeStruct((GROUPS, BASES, WIDTH, WIDTH), F32), field, field),
        in_specs=[anywhere] * 3,
        out_specs=(anywhere,) * 3,
        scratch_shapes=[
            pltpu.VMEM((2, COLS, ROWS, CHAN), BF16),
            pltpu.VMEM((n_lon, 8, CHAN), F32),
            pltpu.VMEM((GROUPS, BASES, WIDTH, WIDTH), F32),
            pltpu.SemaphoreType.DMA((7,)),
            pltpu.SemaphoreType.DMA((7,)),
        ],
        compiler_params=pltpu.CompilerParams(vmem_limit_bytes=56 * 1024 * 1024),
    )(sums, infilled, input_grad)
    return infilled.transpose(1, 0, 2), input_grad.transpose(1, 0, 2), weight_grad


def solution(mesh):
    placed = (P("lat", "lon", None), P("lat", "lon", None), P(), P(), P(), P("lat", "lon", None))
    return jax.shard_map(
        local,
        mesh=mesh,
        in_specs=placed,
        out_specs=(P("lat", "lon", None), P("lat", "lon", None), P()),
        check_vma=False,
    )
```

```python
import functools
import math

import jax
import jax.numpy as jnp
from jax import lax
from jax.experimental import pallas as pl
from jax.experimental.pallas import tpu as pltpu
from jax.sharding import PartitionSpec as P

MESH = pl.DeviceIdType.MESH
F32 = jnp.float32
BF16 = jnp.bfloat16
ROWS = 24
COLS = 45
PADC = 48
SLOT = 64
CHAN = 256
GROUPS = 8
WIDTH = 32
BASES = 4
REACH = 8
TAPS = 2 * REACH + 1
PAIRS = ROWS // 2
BAND = 2 * BASES * PADC


def far_first(sizes):
    steps = [(a, b) for a in range(sizes[0]) for b in range(sizes[1])]
    hops = lambda s: sum(min(k, n - k) for k, n in zip(s, sizes))
    return sorted(steps, key=lambda s: (-hops(s), s))[:-1]


PLANE = far_first((4, 4))
LINE = far_first((2, 8))


def iota(shape, dim):
    return lax.broadcasted_iota(jnp.int32, shape, dim)


def one_hot(test):
    return jnp.where(test, 1.0, 0.0).astype(BF16)


def dot(a, b):
    return jnp.dot(a, b, preferred_element_type=F32)


def pad_rows(x):
    return jnp.concatenate([x, jnp.zeros((PADC - COLS, x.shape[1]), F32)], axis=0)


def kernel(
    n_lat, n_lon,
    feat, mask, taps, width, mix, cot,
    infilled, input_grad, weight_sum,
    feat_own, mask_own, taps_own, mix_own, cot_own,
    wide_feat, wide_cot, tap_rows, base,
    field, seen, cots, cots_t, mixer, band, scaled, pulled, back, total,
    from_right, from_left, marks, marks_right, marks_left, marks_corner, mark_top, mark_bottom,
    corners, share, got_plane, got_line, final,
    send_low, send_high, part_right, part_left, part_top, part_bottom, part_corner,
    load_sem, store_sem, halo_send, halo_recv, part_send, part_recv, sum_send, sum_recv,
):
    la, lo = lax.axis_index("lat"), lax.axis_index("lon")
    up, down = lax.rem(la + n_lat - 1, n_lat), lax.rem(la + 1, n_lat)
    left, right = lax.rem(lo + n_lon - 1, n_lon), lax.rem(lo + 1, n_lon)

    loads = [
        pltpu.make_async_copy(src, dst, load_sem.at[n])
        for n, (src, dst) in enumerate(
            (
                (feat, feat_own), (mask, mask_own), (taps, taps_own),
                (cot, cot_own), (mix, mix_own),
            )
        )
    ]
    for copy in loads:
        copy.start()

    chip_y, core = lax.div(la, 4), lax.rem(la, 2)
    chip_x, chip_z = 2 * lax.rem(lax.div(la, 2), 2) + lax.div(lo, 8), lax.rem(lo, 8)
    plane_rank, line_rank = 4 * chip_y + chip_x, 8 * core + chip_z

    def plane(step):
        y, x = lax.rem(chip_y + step[0], 4), lax.rem(chip_x + step[1], 4)
        return 4 * y + x, (4 * y + 2 * lax.div(x, 2) + core, 8 * lax.rem(x, 2) + chip_z)

    def line_of(step):
        other, z = lax.rem(core + step[0], 2), lax.rem(chip_z + step[1], 8)
        return 8 * other + z, (la - core + other, lo - chip_z + z)

    barrier = pltpu.get_barrier_semaphore()

    def greet(dev_lat, dev_lon):
        pl.semaphore_signal(
            barrier, inc=1, device_id=(dev_lat, dev_lon), device_id_type=MESH
        )

    for dev_lat in (up, down):
        for dev_lon in (left, right):
            greet(dev_lat, dev_lon)

    greet(la, left)
    greet(la, right)
    greet(up, lo)
    greet(down, lo)
    for step in PLANE:
        greet(*plane(step)[1])
    for step in LINE:
        greet(*line_of(step)[1])

    def remote(src, dst, send, recv, dev_lat, dev_lon):
        return pltpu.make_async_remote_copy(
            src_ref=src, dst_ref=dst, send_sem=send, recv_sem=recv,
            device_id=(dev_lat, dev_lon), device_id_type=MESH,
        )

    edge = pl.ds(0, PADC)
    head, tail = pl.ds(0, 16), pl.ds(32, 16)
    halo_plan = (
        (feat_own.at[pl.ds(0, REACH)], from_right, la, left),
        (feat_own.at[pl.ds(COLS - REACH, REACH)], from_left, la, right),
        (marks, marks_right, la, left),
        (marks, marks_left, la, right),
        (mask_own.at[0], mark_bottom, up, lo),
        (mask_own.at[ROWS - 1], mark_top, down, lo),
        (marks, marks_corner.at[0], up, left),
        (marks, marks_corner.at[1], up, right),
        (marks, marks_corner.at[2], down, left),
        (marks, marks_corner.at[3], down, right),
        (field.at[1, edge], field.at[ROWS + 1, edge], up, lo),
        (field.at[ROWS, edge], field.at[0, edge], down, lo),
        (field.at[1, head], corners.at[0], up, left),
        (field.at[1, tail], corners.at[1], up, right),
        (field.at[ROWS, head], corners.at[2], down, left),
        (field.at[ROWS, tail], corners.at[3], down, right),
    )
    halos = [
        remote(src, dst, halo_send.at[n], halo_recv.at[n], dev_lat, dev_lon)
        for n, (src, dst, dev_lat, dev_lon) in enumerate(halo_plan)
    ]

    loads[0].wait()
    pl.semaphore_wait(barrier, 8 + len(PLANE) + len(LINE))
    for copy in halos[0:2]:
        copy.start()

    loads[1].wait()
    flags = mask_own[...].reshape(ROWS * GROUPS, COLS).astype(F32).T.astype(BF16)
    row, col = iota((16, COLS), 0), iota((16, COLS), 1)
    pick = one_hot(col == jnp.where(row < 8, row, row + COLS - 16))
    marks[...] = dot(pick, flags).astype(BF16)
    for copy in halos[2:10]:
        copy.start()

    def widen(ref, n, rows):
        where = pl.ds(pl.multiple_of(ROWS * n, 8), ROWS)
        rows = rows.astype(F32)
        ref[0, where] = rows[:, 0:128]
        ref[1, where] = rows[:, 128:256]

    def cycle_of(ref, i, count):
        where = pl.ds(i, count, stride=ROWS)
        return jnp.concatenate([ref[0, where], ref[1, where]], axis=1)


    @pl.loop(0, COLS, unroll=5)
    def _(n):
        widen(wide_feat, n, feat_own[n])

    def spread(values, i):
        n, k = divmod(i, 16)
        part = values[:, 128 * n : min(128 * n + 128, ROWS * GROUPS)]
        depth = part.shape[1]
        table = one_hot(
            iota((depth, CHAN), 0) == iota((depth, CHAN), 1) // WIDTH + GROUPS * k
        )
        return dot(part, table)

    order = [0, ROWS - 1] + list(range(1, ROWS - 1))
    for i in order:
        wide = spread(flags, i)
        field[i + 1, 0:PADC] = pad_rows(
            cycle_of(wide_feat, i, COLS) * wide
        ).astype(BF16)
        seen[i + 1, 0:PADC] = pad_rows(wide).astype(BF16)
        if i == ROWS - 1:
            for copy in halos[10:]:
                copy.start()

    loads[2].wait()
    cycle = iota((BASES, n_lat * ROWS), 1)
    for a in range(3):
        outside = {0: cycle == 0, 1: cycle < 0, 2: cycle == n_lat * ROWS - 1}[a]
        for e in range(TAPS):
            first = BASES * (TAPS * a + e)
            tap_rows[first : first + BASES] = jnp.where(
                outside, 0.0, taps_own[a, e].astype(F32)
            )
    tap_rows[BASES * 3 * TAPS :] = jnp.zeros((8 - BASES * 3 * TAPS % 8, n_lat * ROWS), F32)
    shape = (ROWS, n_lat * ROWS)
    choose = one_hot(iota(shape, 1) == iota(shape, 0) + la * ROWS)
    mine = lax.dot_general(
        choose, tap_rows[...].astype(BF16), (((1,), (1,)), ((), ())), preferred_element_type=F32
    ).astype(BF16)
    shape = (mine.shape[1], CHAN)
    slot, entry = iota(shape, 1) // SLOT, iota(shape, 1) % SLOT
    odd = iota((ROWS, CHAN), 0) % 2 == 1
    away = jnp.abs(iota((1, CHAN), 1) % SLOT - REACH)
    for b in range(BASES):
        home = (entry < TAPS) & (slot < 3) & (
            iota(shape, 0) == BASES * (TAPS * slot + entry) + b
        )
        line = dot(mine, one_hot(home))
        line = jnp.where(odd, pltpu.roll(line, SLOT, 1), line)
        for i in range(ROWS):
            base[i, b : b + 1] = jnp.where(
                away <= width[la * ROWS + i], line[i : i + 1], 0.0
            )

    lane = iota((PADC, 128), 1) % SLOT

    @pl.loop(0, PAIRS)
    def _(t):
        for k in range(2):
            for b in range(BASES):
                for v in range(2):
                    line = base[2 * t + k, b : b + 1, v * 128 : v * 128 + 128]
                    row = jnp.broadcast_to(line, (PADC, 128))
                    late = pltpu.roll(jnp.broadcast_to(line, (8, 128)), 3, 1)
                    late = jnp.concatenate([late, late], axis=0)
                    own = pltpu.roll(row, 120, 1, stride=1, stride_axis=0)
                    high = pltpu.roll(late, 24, 1, stride=1, stride_axis=0)
                    low = pltpu.roll(row[0:8], 56, 1, stride=1, stride_axis=0)
                    piece = jnp.concatenate(
                        [
                            jnp.where(
                                lane[0:8] < COLS, own[0:8], jnp.where(lane[0:8] < 56, 0.0, low)
                            ),
                            own[8:32],
                            jnp.where(
                                lane[0:16] < COLS,
                                own[32:48],
                                jnp.where(
                                    (lane[0:16] >= PADC) & (lane[0:16] < 56), high, 0.0
                                ),
                            ),
                        ],
                        axis=0,
                    )
                    start = (k * BASES + b) * PADC
                    band[t, start : start + PADC, v * 128 : v * 128 + 128] = piece.astype(BF16)

    loads[3].wait()

    @pl.loop(0, COLS, unroll=5)
    def _(n):
        widen(wide_cot, n, cot_own[n])

    for i in range(ROWS):
        cots[i * PADC : i * PADC + PADC] = pad_rows(
            cycle_of(wide_cot, i, COLS)
        ).astype(BF16)
    for n in range(ROWS * PADC // 128):
        cots_t[:, n * 128 : n * 128 + 128] = cots[n * 128 : n * 128 + 128].T

    loads[4].wait()
    block = iota((CHAN, CHAN), 0) // WIDTH == iota((CHAN, CHAN), 1) // WIDTH
    repeat = one_hot(iota((WIDTH, CHAN), 1) % WIDTH == iota((WIDTH, CHAN), 0))
    for b in range(BASES):
        tall = mix_own[:, b].reshape(CHAN, WIDTH)
        mixer[b] = jnp.where(block, dot(tall, repeat), 0.0).astype(BF16)

    @pl.loop(0, PAIRS // 4)
    def _(n):
        start = pl.multiple_of(n * 8 * PADC, 8 * PADC)
        rows = cots[pl.ds(start, 8 * PADC)]
        for b in range(BASES):
            result = lax.dot_general(
                rows, mixer[b], (((1,), (1,)), ((), ())), preferred_element_type=F32
            )
            for i in range(8):
                first = ((i % 2) * BASES + b) * PADC
                back[4 * n + i // 2, first : first + PADC] = result[i * PADC : i * PADC + PADC]

    for copy in halos[2:]:
        copy.wait_recv()
    upper = iota((16, ROWS * GROUPS), 0) < 8

    def merged(high, low):
        return jnp.where(upper, high.astype(F32), low.astype(F32)).astype(BF16)

    both = merged(marks_right[...], marks_left[...])
    one_row = one_hot(iota((GROUPS, CHAN), 1) // WIDTH == iota((GROUPS, CHAN), 0))
    for i, ref, cycle, high, low in (
        (0, mark_top, ROWS - 1, 2, 3), (ROWS + 1, mark_bottom, 0, 0, 1)
    ):
        flat = dot(ref[...].astype(F32).T.astype(BF16), one_row)
        seen[i, 0:PADC] = pad_rows(flat).astype(BF16)
        pair = merged(marks_corner[high], marks_corner[low])
        seen[i, PADC:SLOT] = spread(pair, cycle).astype(BF16)
        ends = pltpu.roll(corners[low].astype(F32), 11, 0)
        field[i, PADC:SLOT] = jnp.concatenate(
            [corners[high].astype(F32)[0:8], ends[0:8]], axis=0
        ).astype(BF16)
    for copy in halos[0:2]:
        copy.wait_recv()

    @pl.loop(0, REACH, unroll=4)
    def _(n):
        widen(wide_feat, n, from_right[n])
        widen(wide_feat, n + REACH, from_left[n])

    for i in range(ROWS):
        wide = spread(both, i)
        field[i + 1, PADC:SLOT] = (
            cycle_of(wide_feat, i, 2 * REACH) * wide
        ).astype(BF16)
        seen[i + 1, PADC:SLOT] = wide.astype(BF16)

    @pl.loop(0, PAIRS, unroll=4)
    def _(t):
        weights = band[t]
        numerator = dot(weights, field[pl.ds(2 * t, 4)].reshape(4 * SLOT, CHAN))
        denominator = dot(weights, seen[pl.ds(2 * t, 4)].reshape(4 * SLOT, CHAN))
        shrink = 1.0 / jnp.maximum(denominator, 1.0)
        normal = (numerator * shrink).astype(BF16)
        for k in range(2):
            start = pl.multiple_of((2 * t + k) * PADC, PADC)
            for b in range(BASES):
                first = (k * BASES + b) * PADC
                scaled[b, pl.ds(start, PADC)] = normal[first : first + PADC]
        pulled[t] = (back[t] * shrink).astype(BF16)

    for b in range(BASES):
        grad = jnp.where(block, dot(cots_t[...], scaled[b]), 0.0)
        share[b * WIDTH : b * WIDTH + WIDTH] = jnp.sum(grad.reshape(GROUPS, WIDTH, CHAN), axis=0)

    def gather_share(n):
        to, device = plane(PLANE[n])
        rows = pl.ds(pl.multiple_of(to * 8, 8), 8)
        return remote(
            share.at[rows], got_plane.at[n], sum_send.at[0, n], sum_recv.at[0, n], *device
        )

    def swap_share(n):
        _, device = line_of(LINE[n])
        here = got_line.at[line_rank]
        return remote(here, here, sum_send.at[1, n], sum_recv.at[1, n], *device)

    def spread_share(n):
        _, device = plane(PLANE[n])
        return remote(
            final, weight_sum.at[plane_rank], sum_send.at[2, n], sum_recv.at[2, n], *device
        )

    def start_all(make):
        copies = [make(n) for n in range(15)]
        for copy in copies:
            copy.start()
        return copies

    def finish_all(copies):
        for copy in copies:
            copy.wait_recv()

    gathers = start_all(gather_share)

    total[0:2] = jnp.zeros((2, SLOT, CHAN), F32)

    @pl.loop(0, PAIRS, unroll=4)
    def _(t):
        result = dot(band[t].T, pulled[t]).reshape(4, SLOT, CHAN)
        total[pl.ds(2 * t, 2)] += result[0:2]
        total[pl.ds(2 * t + 2, 2)] = result[2:4]

    @pl.loop(0, PAIRS, unroll=4)
    def _(t):
        for ref, first in ((send_high, PADC), (send_low, PADC + 8)):
            ref[t] = jnp.concatenate(
                [total[2 * t + k, first : first + 8] for k in (1, 2)], axis=0
            ).astype(BF16)

    high, low, own = pl.ds(PADC, 8), pl.ds(56, 8), pl.ds(0, PADC)
    part_plan = (
        (send_low, part_right, la, left),
        (send_high, part_left, la, right),
        (total.at[0, own], part_bottom, up, lo),
        (total.at[ROWS + 1, own], part_top, down, lo),
        (total.at[0, low], part_corner.at[0], up, left),
        (total.at[0, high], part_corner.at[1], up, right),
        (total.at[ROWS + 1, low], part_corner.at[2], down, left),
        (total.at[ROWS + 1, high], part_corner.at[3], down, right),
    )
    parts = [
        remote(src, dst, part_send.at[n], part_recv.at[n], dev_lat, dev_lon)
        for n, (src, dst, dev_lat, dev_lon) in enumerate(part_plan)
    ]
    for copy in parts:
        copy.start()

    finish_all(gathers)
    got_line[line_rank] = share[pl.ds(pl.multiple_of(plane_rank * 8, 8), 8)] + jnp.sum(
        got_plane[...], axis=0
    )
    swaps = start_all(swap_share)

    def spill(ref, i, rows):
        where = pl.ds(i, COLS, stride=ROWS)
        ref[0, where] = rows[0:COLS, 0:128]
        ref[1, where] = rows[0:COLS, 128:256]

    def narrow(ref, out):
        @pl.loop(0, COLS, unroll=5)
        def _(n):
            where = pl.ds(pl.multiple_of(ROWS * n, 8), ROWS)
            out[n] = jnp.concatenate([ref[0, where], ref[1, where]], axis=1).astype(BF16)

    @pl.loop(0, PAIRS // 4)
    def _(n):
        start = pl.multiple_of(n * 8 * PADC, 8 * PADC)
        result = dot(scaled[0, pl.ds(start, 8 * PADC)], mixer[0])
        for b in range(1, BASES):
            result += dot(scaled[b, pl.ds(start, 8 * PADC)], mixer[b])
        for i in range(8):
            spill(wide_cot, 8 * n + i, result[i * PADC : i * PADC + PADC])

    narrow(wide_cot, cot_own)
    stores = [pltpu.make_async_copy(cot_own, infilled, store_sem.at[0])]
    stores[0].start()

    finish_all(swaps)
    final[...] = jnp.sum(got_line[...], axis=0) * (
        1.0 / math.sqrt(ROWS * n_lat * COLS * n_lon)
    )
    spreads = start_all(spread_share)
    stores.append(pltpu.make_async_copy(final, weight_sum.at[plane_rank], store_sem.at[2]))
    stores[1].start()

    for copy in halos:
        copy.wait_send()
    for copy in parts:
        copy.wait_recv()
    for copy in parts:
        copy.wait_send()

    def at_end(strip):
        return pltpu.roll(jnp.concatenate([strip, jnp.zeros((8, CHAN), F32)], axis=0), 5, 0)

    total[1, 0:PADC] += part_top[...]
    total[ROWS, 0:PADC] += part_bottom[...]
    for i, first, last in ((1, 3, 2), (ROWS, 1, 0)):
        total[i, 0:8] += part_corner[first]
        total[i, 32:PADC] += at_end(part_corner[last])

    @pl.loop(0, PAIRS, unroll=2)
    def _(t):
        before, after = part_left[t].astype(F32), part_right[t].astype(F32)
        for k in range(2):
            i, rows = 2 * t + k, slice(8 * k, 8 * k + 8)
            extra = jnp.concatenate(
                [before[rows], jnp.zeros((24, CHAN), F32), at_end(after[rows])], axis=0
            )
            result = (total[i + 1, 0:PADC] + extra) * seen[i + 1, 0:PADC].astype(F32)
            spill(wide_feat, i, result)

    narrow(wide_feat, feat_own)
    stores.append(pltpu.make_async_copy(feat_own, input_grad, store_sem.at[1]))
    stores[2].start()

    for copy in gathers + swaps:
        copy.wait_send()

    finish_all(spreads)
    for copy in spreads:
        copy.wait_send()
    for copy in stores:
        copy.wait()


def finish(
    sums, first, second, grads, first_out, second_out, held, sums_own, grads_own, in_sem, out_sem
):
    load_sums = pltpu.make_async_copy(sums, sums_own, in_sem.at[6])
    load_sums.start()
    step = COLS // 3
    loads, stores = [], []
    for n, (src, dst) in enumerate(((first, first_out), (second, second_out))):
        for k in range(3):
            part = pl.ds(k * step, step)
            loads.append(
                pltpu.make_async_copy(src.at[part], held.at[n, part], in_sem.at[3 * n + k])
            )
            stores.append(
                pltpu.make_async_copy(held.at[n, part], dst.at[part], out_sem.at[3 * n + k])
            )
    for copy in loads:
        copy.start()
    load_sums.wait()
    for b in range(BASES):
        grad = sums_own[4 * b : 4 * b + 4].reshape(WIDTH, CHAN)
        grads_own[:, b] = grad.T.reshape(GROUPS, WIDTH, WIDTH)
    stores.append(pltpu.make_async_copy(grads_own, grads, out_sem.at[6]))
    stores[6].start()
    for load, store in zip(loads, stores):
        load.wait()
        store.start()
    for copy in stores:
        copy.wait()


def local(features, obs_mask, filter_taps, band_width, mixing, cotangent):
    n_lat, n_lon = lax.axis_size("lat"), lax.axis_size("lon")
    anywhere = pl.BlockSpec(memory_space=pltpu.HBM)
    marks = pltpu.VMEM((16, ROWS * GROUPS), BF16)
    strips = pltpu.VMEM((PAIRS, 16, CHAN), BF16)
    field = jax.ShapeDtypeStruct((COLS, ROWS, CHAN), BF16)
    infilled, input_grad, sums = pl.pallas_call(
        functools.partial(kernel, n_lat, n_lon),
        out_shape=(
            field,
            field,
            jax.ShapeDtypeStruct((n_lon, 8, CHAN), F32),
        ),
        in_specs=[anywhere] * 3 + [pl.BlockSpec(memory_space=pltpu.SMEM)] + [anywhere] * 2,
        out_specs=(anywhere,) * 3,
        scratch_shapes=[
            pltpu.VMEM((COLS, ROWS, CHAN), BF16),
            pltpu.VMEM((ROWS, GROUPS, COLS), jnp.int32),
            pltpu.VMEM((3, TAPS, BASES, n_lat * ROWS), BF16),
            pltpu.VMEM((GROUPS, BASES, WIDTH, WIDTH), BF16),
            pltpu.VMEM((COLS, ROWS, CHAN), BF16),
            pltpu.VMEM((2, COLS * ROWS, 128), F32),
            pltpu.VMEM((2, COLS * ROWS, 128), F32),
            pltpu.VMEM((208, n_lat * ROWS), F32),
            pltpu.VMEM((ROWS, BASES, CHAN), F32),
            pltpu.VMEM((ROWS + 2, SLOT, CHAN), BF16),
            pltpu.VMEM((ROWS + 2, SLOT, CHAN), BF16),
            pltpu.VMEM((ROWS * PADC, CHAN), BF16),
            pltpu.VMEM((CHAN, ROWS * PADC), BF16),
            pltpu.VMEM((BASES, CHAN, CHAN), BF16),
            pltpu.VMEM((PAIRS, BAND, 4 * SLOT), BF16),
            pltpu.VMEM((BASES, ROWS * PADC, CHAN), BF16),
            pltpu.VMEM((PAIRS, BAND, CHAN), BF16),
            pltpu.VMEM((PAIRS, BAND, CHAN), F32),
            pltpu.VMEM((ROWS + 2, SLOT, CHAN), F32),
            pltpu.VMEM((REACH, ROWS, CHAN), BF16),
            pltpu.VMEM((REACH, ROWS, CHAN), BF16),
            marks, marks, marks,
            pltpu.VMEM((4, 16, ROWS * GROUPS), BF16),
            pltpu.VMEM((GROUPS, COLS), jnp.int32),
            pltpu.VMEM((GROUPS, COLS), jnp.int32),
            pltpu.VMEM((4, 16, CHAN), BF16),
            pltpu.VMEM((BASES * WIDTH, CHAN), F32),
            pltpu.VMEM((15, 8, CHAN), F32),
            pltpu.VMEM((16, 8, CHAN), F32),
            pltpu.VMEM((8, CHAN), F32),
            strips, strips, strips, strips,
            pltpu.VMEM((PADC, CHAN), F32),
            pltpu.VMEM((PADC, CHAN), F32),
            pltpu.VMEM((4, 8, CHAN), F32),
            pltpu.SemaphoreType.DMA((5,)),
            pltpu.SemaphoreType.DMA((3,)),
            pltpu.SemaphoreType.DMA((16,)),
            pltpu.SemaphoreType.DMA((16,)),
            pltpu.SemaphoreType.DMA((8,)),
            pltpu.SemaphoreType.DMA((8,)),
            pltpu.SemaphoreType.DMA((3, 16)),
            pltpu.SemaphoreType.DMA((3, 16)),
        ],
        compiler_params=pltpu.CompilerParams(
            collective_id=0, has_side_effects=True, vmem_limit_bytes=56 * 1024 * 1024
        ),
    )(
        features.transpose(1, 0, 2),
        obs_mask.transpose(0, 2, 1),
        filter_taps.transpose(2, 3, 1, 0),
        band_width,
        mixing,
        cotangent.transpose(1, 0, 2),
    )
    weight_grad, infilled, input_grad = pl.pallas_call(
        finish,
        out_shape=(jax.ShapeDtypeStruct((GROUPS, BASES, WIDTH, WIDTH), F32), field, field),
        in_specs=[anywhere] * 3,
        out_specs=(anywhere,) * 3,
        scratch_shapes=[
            pltpu.VMEM((2, COLS, ROWS, CHAN), BF16),
            pltpu.VMEM((n_lon, 8, CHAN), F32),
            pltpu.VMEM((GROUPS, BASES, WIDTH, WIDTH), F32),
            pltpu.SemaphoreType.DMA((7,)),
            pltpu.SemaphoreType.DMA((7,)),
        ],
        compiler_params=pltpu.CompilerParams(vmem_limit_bytes=56 * 1024 * 1024),
    )(sums, infilled, input_grad)
    return infilled.transpose(1, 0, 2), input_grad.transpose(1, 0, 2), weight_grad


def solution(mesh):
    placed = (P("lat", "lon", None), P("lat", "lon", None), P(), P(), P(), P("lat", "lon", None))
    return jax.shard_map(
        local,
        mesh=mesh,
        in_specs=placed,
        out_specs=(P("lat", "lon", None), P("lat", "lon", None), P()),
        check_vma=False,
    )
```

```python
import functools
import math

import jax
import jax.numpy as jnp
from jax import lax
from jax.experimental import pallas as pl
from jax.experimental.pallas import tpu as pltpu
from jax.sharding import PartitionSpec as P

MESH = pl.DeviceIdType.MESH
F32 = jnp.float32
BF16 = jnp.bfloat16
ROWS = 24
COLS = 45
PADC = 48
SLOT = 64
CHAN = 256
GROUPS = 8
WIDTH = 32
BASES = 4
REACH = 8
TAPS = 2 * REACH + 1
PAIRS = ROWS // 2
BAND = 2 * BASES * PADC


def far_first(sizes):
    steps = [(a, b) for a in range(sizes[0]) for b in range(sizes[1])]
    hops = lambda s: sum(min(k, n - k) for k, n in zip(s, sizes))
    return sorted(steps, key=lambda s: (-hops(s), s))[:-1]


PLANE = far_first((4, 4))
LINE = far_first((2, 8))


def iota(shape, dim):
    return lax.broadcasted_iota(jnp.int32, shape, dim)


def one_hot(test):
    return jnp.where(test, 1.0, 0.0).astype(BF16)


def dot(a, b):
    return jnp.dot(a, b, preferred_element_type=F32)


def pad_rows(x):
    return jnp.concatenate([x, jnp.zeros((PADC - COLS, x.shape[1]), F32)], axis=0)


def kernel(
    n_lat, n_lon,
    feat, mask, taps, width, mix, cot,
    infilled, input_grad, weight_sum,
    feat_own, mask_own, taps_own, mix_own, cot_own,
    wide_feat, wide_cot, tap_rows, base,
    field, seen, cots, cots_t, mixer, band, scaled, pulled, back, total,
    from_right, from_left, marks, marks_right, marks_left, marks_corner, mark_top, mark_bottom,
    corners, share, got_plane, got_line, final,
    send_low, send_high, part_right, part_left, part_top, part_bottom, part_corner,
    load_sem, store_sem, halo_send, halo_recv, part_send, part_recv, sum_send, sum_recv,
):
    la, lo = lax.axis_index("lat"), lax.axis_index("lon")
    up, down = lax.rem(la + n_lat - 1, n_lat), lax.rem(la + 1, n_lat)
    left, right = lax.rem(lo + n_lon - 1, n_lon), lax.rem(lo + 1, n_lon)

    loads = [
        pltpu.make_async_copy(src, dst, load_sem.at[n])
        for n, (src, dst) in enumerate(
            (
                (feat, feat_own), (mask, mask_own), (taps, taps_own),
                (cot, cot_own), (mix, mix_own),
            )
        )
    ]
    for copy in loads:
        copy.start()

    chip_y, core = lax.div(la, 4), lax.rem(la, 2)
    chip_x, chip_z = 2 * lax.rem(lax.div(la, 2), 2) + lax.div(lo, 8), lax.rem(lo, 8)
    plane_rank, line_rank = 4 * chip_y + chip_x, 8 * core + chip_z

    def plane(step):
        y, x = lax.rem(chip_y + step[0], 4), lax.rem(chip_x + step[1], 4)
        return 4 * y + x, (4 * y + 2 * lax.div(x, 2) + core, 8 * lax.rem(x, 2) + chip_z)

    def line_of(step):
        other, z = lax.rem(core + step[0], 2), lax.rem(chip_z + step[1], 8)
        return 8 * other + z, (la - core + other, lo - chip_z + z)

    barrier = pltpu.get_barrier_semaphore()

    def greet(dev_lat, dev_lon):
        pl.semaphore_signal(
            barrier, inc=1, device_id=(dev_lat, dev_lon), device_id_type=MESH
        )

    for dev_lat in (up, down):
        for dev_lon in (left, right):
            greet(dev_lat, dev_lon)

    greet(la, left)
    greet(la, right)
    greet(up, lo)
    greet(down, lo)
    for step in PLANE:
        greet(*plane(step)[1])
    for step in LINE:
        greet(*line_of(step)[1])

    def remote(src, dst, send, recv, dev_lat, dev_lon):
        return pltpu.make_async_remote_copy(
            src_ref=src, dst_ref=dst, send_sem=send, recv_sem=recv,
            device_id=(dev_lat, dev_lon), device_id_type=MESH,
        )

    edge = pl.ds(0, PADC)
    head, tail = pl.ds(0, 16), pl.ds(32, 16)
    halo_plan = (
        (feat_own.at[pl.ds(0, REACH)], from_right, la, left),
        (feat_own.at[pl.ds(COLS - REACH, REACH)], from_left, la, right),
        (marks, marks_right, la, left),
        (marks, marks_left, la, right),
        (mask_own.at[0], mark_bottom, up, lo),
        (mask_own.at[ROWS - 1], mark_top, down, lo),
        (marks, marks_corner.at[0], up, left),
        (marks, marks_corner.at[1], up, right),
        (marks, marks_corner.at[2], down, left),
        (marks, marks_corner.at[3], down, right),
        (field.at[1, edge], field.at[ROWS + 1, edge], up, lo),
        (field.at[ROWS, edge], field.at[0, edge], down, lo),
        (field.at[1, head], corners.at[0], up, left),
        (field.at[1, tail], corners.at[1], up, right),
        (field.at[ROWS, head], corners.at[2], down, left),
        (field.at[ROWS, tail], corners.at[3], down, right),
    )
    halos = [
        remote(src, dst, halo_send.at[n], halo_recv.at[n], dev_lat, dev_lon)
        for n, (src, dst, dev_lat, dev_lon) in enumerate(halo_plan)
    ]

    loads[0].wait()
    pl.semaphore_wait(barrier, 8 + len(PLANE) + len(LINE))
    for copy in halos[0:2]:
        copy.start()

    loads[1].wait()
    flags = mask_own[...].reshape(ROWS * GROUPS, COLS).astype(F32).T.astype(BF16)
    row, col = iota((16, COLS), 0), iota((16, COLS), 1)
    pick = one_hot(col == jnp.where(row < 8, row, row + COLS - 16))
    marks[...] = dot(pick, flags).astype(BF16)
    for copy in halos[2:10]:
        copy.start()

    def widen(ref, n, rows):
        where = pl.ds(pl.multiple_of(ROWS * n, 8), ROWS)
        rows = rows.astype(F32)
        ref[0, where] = rows[:, 0:128]
        ref[1, where] = rows[:, 128:256]

    def cycle_of(ref, i, count):
        where = pl.ds(i, count, stride=ROWS)
        return jnp.concatenate([ref[0, where], ref[1, where]], axis=1)


    @pl.loop(0, COLS, unroll=5)
    def _(n):
        widen(wide_feat, n, feat_own[n])

    def spread(values, i):
        n, k = divmod(i, 16)
        part = values[:, 128 * n : min(128 * n + 128, ROWS * GROUPS)]
        depth = part.shape[1]
        table = one_hot(
            iota((depth, CHAN), 0) == iota((depth, CHAN), 1) // WIDTH + GROUPS * k
        )
        return dot(part, table)

    order = [0, ROWS - 1] + list(range(1, ROWS - 1))
    for i in order:
        wide = spread(flags, i)
        field[i + 1, 0:PADC] = pad_rows(
            cycle_of(wide_feat, i, COLS) * wide
        ).astype(BF16)
        seen[i + 1, 0:PADC] = pad_rows(wide).astype(BF16)
        if i == ROWS - 1:
            for copy in halos[10:]:
                copy.start()

    loads[2].wait()
    cycle = iota((BASES, n_lat * ROWS), 1)
    for a in range(3):
        outside = {0: cycle == 0, 1: cycle < 0, 2: cycle == n_lat * ROWS - 1}[a]
        for e in range(TAPS):
            first = BASES * (TAPS * a + e)
            tap_rows[first : first + BASES] = jnp.where(
                outside, 0.0, taps_own[a, e].astype(F32)
            )
    tap_rows[BASES * 3 * TAPS :] = jnp.zeros((8 - BASES * 3 * TAPS % 8, n_lat * ROWS), F32)
    shape = (ROWS, n_lat * ROWS)
    choose = one_hot(iota(shape, 1) == iota(shape, 0) + la * ROWS)
    mine = lax.dot_general(
        choose, tap_rows[...].astype(BF16), (((1,), (1,)), ((), ())), preferred_element_type=F32
    ).astype(BF16)
    shape = (mine.shape[1], CHAN)
    slot, entry = iota(shape, 1) // SLOT, iota(shape, 1) % SLOT
    odd = iota((ROWS, CHAN), 0) % 2 == 1
    away = jnp.abs(iota((1, CHAN), 1) % SLOT - REACH)
    for b in range(BASES):
        home = (entry < TAPS) & (slot < 3) & (
            iota(shape, 0) == BASES * (TAPS * slot + entry) + b
        )
        line = dot(mine, one_hot(home))
        line = jnp.where(odd, pltpu.roll(line, SLOT, 1), line)
        for i in range(ROWS):
            base[i, b : b + 1] = jnp.where(
                away <= width[la * ROWS + i], line[i : i + 1], 0.0
            )

    lane = iota((PADC, 128), 1) % SLOT

    @pl.loop(0, PAIRS)
    def _(t):
        for k in range(2):
            for b in range(BASES):
                for v in range(2):
                    line = base[2 * t + k, b : b + 1, v * 128 : v * 128 + 128]
                    row = jnp.broadcast_to(line, (PADC, 128))
                    late = pltpu.roll(jnp.broadcast_to(line, (8, 128)), 3, 1)
                    late = jnp.concatenate([late, late], axis=0)
                    own = pltpu.roll(row, 120, 1, stride=1, stride_axis=0)
                    high = pltpu.roll(late, 24, 1, stride=1, stride_axis=0)
                    low = pltpu.roll(row[0:8], 56, 1, stride=1, stride_axis=0)
                    piece = jnp.concatenate(
                        [
                            jnp.where(
                                lane[0:8] < COLS, own[0:8], jnp.where(lane[0:8] < 56, 0.0, low)
                            ),
                            own[8:32],
                            jnp.where(
                                lane[0:16] < COLS,
                                own[32:48],
                                jnp.where(
                                    (lane[0:16] >= PADC) & (lane[0:16] < 56), high, 0.0
                                ),
                            ),
                        ],
                        axis=0,
                    )
                    start = (k * BASES + b) * PADC
                    band[t, start : start + PADC, v * 128 : v * 128 + 128] = piece.astype(BF16)

    loads[3].wait()

    @pl.loop(0, COLS, unroll=5)
    def _(n):
        widen(wide_cot, n, cot_own[n])

    for i in range(ROWS):
        cots[i * PADC : i * PADC + PADC] = pad_rows(
            cycle_of(wide_cot, i, COLS)
        ).astype(BF16)
    for n in range(ROWS * PADC // 128):
        cots_t[:, n * 128 : n * 128 + 128] = cots[n * 128 : n * 128 + 128].T

    loads[4].wait()
    block = iota((CHAN, CHAN), 0) // WIDTH == iota((CHAN, CHAN), 1) // WIDTH
    repeat = one_hot(iota((WIDTH, CHAN), 1) % WIDTH == iota((WIDTH, CHAN), 0))
    for b in range(BASES):
        tall = mix_own[:, b].reshape(CHAN, WIDTH)
        mixer[b] = jnp.where(block, dot(tall, repeat), 0.0).astype(BF16)

    @pl.loop(0, PAIRS // 4)
    def _(n):
        start = pl.multiple_of(n * 8 * PADC, 8 * PADC)
        rows = cots[pl.ds(start, 8 * PADC)]
        for b in range(BASES):
            result = lax.dot_general(
                rows, mixer[b], (((1,), (1,)), ((), ())), preferred_element_type=F32
            )
            for i in range(8):
                first = ((i % 2) * BASES + b) * PADC
                back[4 * n + i // 2, first : first + PADC] = result[i * PADC : i * PADC + PADC]

    for copy in halos[2:]:
        copy.wait_recv()
    upper = iota((16, ROWS * GROUPS), 0) < 8

    def merged(high, low):
        return jnp.where(upper, high.astype(F32), low.astype(F32)).astype(BF16)

    both = merged(marks_right[...], marks_left[...])
    one_row = one_hot(iota((GROUPS, CHAN), 1) // WIDTH == iota((GROUPS, CHAN), 0))
    for i, ref, cycle, high, low in (
        (0, mark_top, ROWS - 1, 2, 3), (ROWS + 1, mark_bottom, 0, 0, 1)
    ):
        flat = dot(ref[...].astype(F32).T.astype(BF16), one_row)
        seen[i, 0:PADC] = pad_rows(flat).astype(BF16)
        pair = merged(marks_corner[high], marks_corner[low])
        seen[i, PADC:SLOT] = spread(pair, cycle).astype(BF16)
        ends = pltpu.roll(corners[low].astype(F32), 11, 0)
        field[i, PADC:SLOT] = jnp.concatenate(
            [corners[high].astype(F32)[0:8], ends[0:8]], axis=0
        ).astype(BF16)
    for copy in halos[0:2]:
        copy.wait_recv()

    @pl.loop(0, REACH, unroll=4)
    def _(n):
        widen(wide_feat, n, from_right[n])
        widen(wide_feat, n + REACH, from_left[n])

    for i in range(ROWS):
        wide = spread(both, i)
        field[i + 1, PADC:SLOT] = (
            cycle_of(wide_feat, i, 2 * REACH) * wide
        ).astype(BF16)
        seen[i + 1, PADC:SLOT] = wide.astype(BF16)

    @pl.loop(0, PAIRS, unroll=4)
    def _(t):
        weights = band[t]
        numerator = dot(weights, field[pl.ds(2 * t, 4)].reshape(4 * SLOT, CHAN))
        denominator = dot(weights, seen[pl.ds(2 * t, 4)].reshape(4 * SLOT, CHAN))
        shrink = 1.0 / jnp.maximum(denominator, 1.0)
        normal = (numerator * shrink).astype(BF16)
        for k in range(2):
            start = pl.multiple_of((2 * t + k) * PADC, PADC)
            for b in range(BASES):
                first = (k * BASES + b) * PADC
                scaled[b, pl.ds(start, PADC)] = normal[first : first + PADC]
        pulled[t] = (back[t] * shrink).astype(BF16)

    def gather_share(n):
        to, device = plane(PLANE[n])
        rows = pl.ds(pl.multiple_of(to * 8, 8), 8)
        return remote(
            share.at[rows], got_plane.at[n], sum_send.at[0, n], sum_recv.at[0, n], *device
        )

    def swap_share(n):
        _, device = line_of(LINE[n])
        here = got_line.at[line_rank]
        return remote(here, here, sum_send.at[1, n], sum_recv.at[1, n], *device)

    def spread_share(n):
        _, device = plane(PLANE[n])
        return remote(
            final, weight_sum.at[plane_rank], sum_send.at[2, n], sum_recv.at[2, n], *device
        )

    def start_all(make):
        copies = [make(n) for n in range(15)]
        for copy in copies:
            copy.start()
        return copies

    def finish_all(copies):
        for copy in copies:
            copy.wait_recv()

    gathers = []
    for away_y in (2, 1, 3, 0):
        b = lax.rem(chip_y + away_y, BASES)
        grad = jnp.where(block, dot(cots_t[...], scaled[b]), 0.0)
        rows = pl.ds(pl.multiple_of(b * WIDTH, WIDTH), WIDTH)
        share[rows] = jnp.sum(grad.reshape(GROUPS, WIDTH, CHAN), axis=0)
        for n, step in enumerate(PLANE):
            if step[0] == away_y:
                gathers.append(gather_share(n))
                gathers[-1].start()

    total[0:2] = jnp.zeros((2, SLOT, CHAN), F32)

    @pl.loop(0, PAIRS, unroll=4)
    def _(t):
        result = dot(band[t].T, pulled[t]).reshape(4, SLOT, CHAN)
        total[pl.ds(2 * t, 2)] += result[0:2]
        total[pl.ds(2 * t + 2, 2)] = result[2:4]

    @pl.loop(0, PAIRS, unroll=4)
    def _(t):
        for ref, first in ((send_high, PADC), (send_low, PADC + 8)):
            ref[t] = jnp.concatenate(
                [total[2 * t + k, first : first + 8] for k in (1, 2)], axis=0
            ).astype(BF16)

    high, low, own = pl.ds(PADC, 8), pl.ds(56, 8), pl.ds(0, PADC)
    part_plan = (
        (send_low, part_right, la, left),
        (send_high, part_left, la, right),
        (total.at[0, own], part_bottom, up, lo),
        (total.at[ROWS + 1, own], part_top, down, lo),
        (total.at[0, low], part_corner.at[0], up, left),
        (total.at[0, high], part_corner.at[1], up, right),
        (total.at[ROWS + 1, low], part_corner.at[2], down, left),
        (total.at[ROWS + 1, high], part_corner.at[3], down, right),
    )
    parts = [
        remote(src, dst, part_send.at[n], part_recv.at[n], dev_lat, dev_lon)
        for n, (src, dst, dev_lat, dev_lon) in enumerate(part_plan)
    ]
    for copy in parts:
        copy.start()

    finish_all(gathers)
    got_line[line_rank] = share[pl.ds(pl.multiple_of(plane_rank * 8, 8), 8)] + jnp.sum(
        got_plane[...], axis=0
    )
    swaps = start_all(swap_share)

    def spill(ref, i, rows):
        where = pl.ds(i, COLS, stride=ROWS)
        ref[0, where] = rows[0:COLS, 0:128]
        ref[1, where] = rows[0:COLS, 128:256]

    def narrow(ref, out):
        @pl.loop(0, COLS, unroll=5)
        def _(n):
            where = pl.ds(pl.multiple_of(ROWS * n, 8), ROWS)
            out[n] = jnp.concatenate([ref[0, where], ref[1, where]], axis=1).astype(BF16)

    @pl.loop(0, PAIRS // 4)
    def _(n):
        start = pl.multiple_of(n * 8 * PADC, 8 * PADC)
        result = dot(scaled[0, pl.ds(start, 8 * PADC)], mixer[0])
        for b in range(1, BASES):
            result += dot(scaled[b, pl.ds(start, 8 * PADC)], mixer[b])
        for i in range(8):
            spill(wide_cot, 8 * n + i, result[i * PADC : i * PADC + PADC])

    narrow(wide_cot, cot_own)
    stores = [pltpu.make_async_copy(cot_own, infilled, store_sem.at[0])]
    stores[0].start()

    finish_all(swaps)
    final[...] = jnp.sum(got_line[...], axis=0) * (
        1.0 / math.sqrt(ROWS * n_lat * COLS * n_lon)
    )
    spreads = start_all(spread_share)
    stores.append(pltpu.make_async_copy(final, weight_sum.at[plane_rank], store_sem.at[2]))
    stores[1].start()

    for copy in halos:
        copy.wait_send()
    for copy in parts:
        copy.wait_recv()
    for copy in parts:
        copy.wait_send()

    def at_end(strip):
        return pltpu.roll(jnp.concatenate([strip, jnp.zeros((8, CHAN), F32)], axis=0), 5, 0)

    total[1, 0:PADC] += part_top[...]
    total[ROWS, 0:PADC] += part_bottom[...]
    for i, first, last in ((1, 3, 2), (ROWS, 1, 0)):
        total[i, 0:8] += part_corner[first]
        total[i, 32:PADC] += at_end(part_corner[last])

    @pl.loop(0, PAIRS, unroll=2)
    def _(t):
        before, after = part_left[t].astype(F32), part_right[t].astype(F32)
        for k in range(2):
            i, rows = 2 * t + k, slice(8 * k, 8 * k + 8)
            extra = jnp.concatenate(
                [before[rows], jnp.zeros((24, CHAN), F32), at_end(after[rows])], axis=0
            )
            result = (total[i + 1, 0:PADC] + extra) * seen[i + 1, 0:PADC].astype(F32)
            spill(wide_feat, i, result)

    narrow(wide_feat, feat_own)
    stores.append(pltpu.make_async_copy(feat_own, input_grad, store_sem.at[1]))
    stores[2].start()

    for copy in gathers + swaps:
        copy.wait_send()

    finish_all(spreads)
    for copy in spreads:
        copy.wait_send()
    for copy in stores:
        copy.wait()


def finish(
    sums, first, second, grads, first_out, second_out, held, sums_own, grads_own, in_sem, out_sem
):
    load_sums = pltpu.make_async_copy(sums, sums_own, in_sem.at[6])
    load_sums.start()
    step = COLS // 3
    loads, stores = [], []
    for n, (src, dst) in enumerate(((first, first_out), (second, second_out))):
        for k in range(3):
            part = pl.ds(k * step, step)
            loads.append(
                pltpu.make_async_copy(src.at[part], held.at[n, part], in_sem.at[3 * n + k])
            )
            stores.append(
                pltpu.make_async_copy(held.at[n, part], dst.at[part], out_sem.at[3 * n + k])
            )
    for copy in loads:
        copy.start()
    load_sums.wait()
    for b in range(BASES):
        grad = sums_own[4 * b : 4 * b + 4].reshape(WIDTH, CHAN)
        grads_own[:, b] = grad.T.reshape(GROUPS, WIDTH, WIDTH)
    stores.append(pltpu.make_async_copy(grads_own, grads, out_sem.at[6]))
    stores[6].start()
    for load, store in zip(loads, stores):
        load.wait()
        store.start()
    for copy in stores:
        copy.wait()


def local(features, obs_mask, filter_taps, band_width, mixing, cotangent):
    n_lat, n_lon = lax.axis_size("lat"), lax.axis_size("lon")
    anywhere = pl.BlockSpec(memory_space=pltpu.HBM)
    marks = pltpu.VMEM((16, ROWS * GROUPS), BF16)
    strips = pltpu.VMEM((PAIRS, 16, CHAN), BF16)
    field = jax.ShapeDtypeStruct((COLS, ROWS, CHAN), BF16)
    infilled, input_grad, sums = pl.pallas_call(
        functools.partial(kernel, n_lat, n_lon),
        out_shape=(
            field,
            field,
            jax.ShapeDtypeStruct((n_lon, 8, CHAN), F32),
        ),
        in_specs=[anywhere] * 3 + [pl.BlockSpec(memory_space=pltpu.SMEM)] + [anywhere] * 2,
        out_specs=(anywhere,) * 3,
        scratch_shapes=[
            pltpu.VMEM((COLS, ROWS, CHAN), BF16),
            pltpu.VMEM((ROWS, GROUPS, COLS), jnp.int32),
            pltpu.VMEM((3, TAPS, BASES, n_lat * ROWS), BF16),
            pltpu.VMEM((GROUPS, BASES, WIDTH, WIDTH), BF16),
            pltpu.VMEM((COLS, ROWS, CHAN), BF16),
            pltpu.VMEM((2, COLS * ROWS, 128), F32),
            pltpu.VMEM((2, COLS * ROWS, 128), F32),
            pltpu.VMEM((208, n_lat * ROWS), F32),
            pltpu.VMEM((ROWS, BASES, CHAN), F32),
            pltpu.VMEM((ROWS + 2, SLOT, CHAN), BF16),
            pltpu.VMEM((ROWS + 2, SLOT, CHAN), BF16),
            pltpu.VMEM((ROWS * PADC, CHAN), BF16),
            pltpu.VMEM((CHAN, ROWS * PADC), BF16),
            pltpu.VMEM((BASES, CHAN, CHAN), BF16),
            pltpu.VMEM((PAIRS, BAND, 4 * SLOT), BF16),
            pltpu.VMEM((BASES, ROWS * PADC, CHAN), BF16),
            pltpu.VMEM((PAIRS, BAND, CHAN), BF16),
            pltpu.VMEM((PAIRS, BAND, CHAN), F32),
            pltpu.VMEM((ROWS + 2, SLOT, CHAN), F32),
            pltpu.VMEM((REACH, ROWS, CHAN), BF16),
            pltpu.VMEM((REACH, ROWS, CHAN), BF16),
            marks, marks, marks,
            pltpu.VMEM((4, 16, ROWS * GROUPS), BF16),
            pltpu.VMEM((GROUPS, COLS), jnp.int32),
            pltpu.VMEM((GROUPS, COLS), jnp.int32),
            pltpu.VMEM((4, 16, CHAN), BF16),
            pltpu.VMEM((BASES * WIDTH, CHAN), F32),
            pltpu.VMEM((15, 8, CHAN), F32),
            pltpu.VMEM((16, 8, CHAN), F32),
            pltpu.VMEM((8, CHAN), F32),
            strips, strips, strips, strips,
            pltpu.VMEM((PADC, CHAN), F32),
            pltpu.VMEM((PADC, CHAN), F32),
            pltpu.VMEM((4, 8, CHAN), F32),
            pltpu.SemaphoreType.DMA((5,)),
            pltpu.SemaphoreType.DMA((3,)),
            pltpu.SemaphoreType.DMA((16,)),
            pltpu.SemaphoreType.DMA((16,)),
            pltpu.SemaphoreType.DMA((8,)),
            pltpu.SemaphoreType.DMA((8,)),
            pltpu.SemaphoreType.DMA((3, 16)),
            pltpu.SemaphoreType.DMA((3, 16)),
        ],
        compiler_params=pltpu.CompilerParams(
            collective_id=0, has_side_effects=True, vmem_limit_bytes=56 * 1024 * 1024
        ),
    )(
        features.transpose(1, 0, 2),
        obs_mask.transpose(0, 2, 1),
        filter_taps.transpose(2, 3, 1, 0),
        band_width,
        mixing,
        cotangent.transpose(1, 0, 2),
    )
    weight_grad, infilled, input_grad = pl.pallas_call(
        finish,
        out_shape=(jax.ShapeDtypeStruct((GROUPS, BASES, WIDTH, WIDTH), F32), field, field),
        in_specs=[anywhere] * 3,
        out_specs=(anywhere,) * 3,
        scratch_shapes=[
            pltpu.VMEM((2, COLS, ROWS, CHAN), BF16),
            pltpu.VMEM((n_lon, 8, CHAN), F32),
            pltpu.VMEM((GROUPS, BASES, WIDTH, WIDTH), F32),
            pltpu.SemaphoreType.DMA((7,)),
            pltpu.SemaphoreType.DMA((7,)),
        ],
        compiler_params=pltpu.CompilerParams(vmem_limit_bytes=56 * 1024 * 1024),
    )(sums, infilled, input_grad)
    return infilled.transpose(1, 0, 2), input_grad.transpose(1, 0, 2), weight_grad


def solution(mesh):
    placed = (P("lat", "lon", None), P("lat", "lon", None), P(), P(), P(), P("lat", "lon", None))
    return jax.shard_map(
        local,
        mesh=mesh,
        in_specs=placed,
        out_specs=(P("lat", "lon", None), P("lat", "lon", None), P()),
        check_vma=False,
    )
```
